32 devices in a mesh: ctx: 8 (over y, x, core), tp: 4 (over z).
Axes of the slice: x: 2, y: 2, z: 4, core: 2. Of those that a mesh axis runs over, the one named last changes fastest.
Arguments:
- hidden: bfloat16 [4096, 8192], P('ctx', 'tp'), may hold values from -6 to 6
- queries: bfloat16 [4096, 8192], P('ctx', 'tp'), may hold values from -6.5 to 6.5
- rotated_keys: bfloat16 [4096, 1024], P('ctx', 'tp'), may hold values from -6 to 6
- frozen_value_rows: bfloat16 [4096, 1024], P('ctx', 'tp'), may hold values from -6 to 6
- adapter_a_v: bfloat16 [8192, 16], P('tp'), may hold values from -0.0625 to 0.0625
- value_up_matrix: bfloat16 [16, 1024], P(None, 'tp'), may hold values from -1.5 to 1.5
- adapter_a_o: bfloat16 [8192, 16], P('tp'), may hold values from -0.0625 to 0.0625
- output_up_matrix: bfloat16 [16, 8192], P(None, 'tp'), may hold values from -1.5 to 1.5
- doc_lengths: int32 [16], replicated, may hold values from 1 to 1536, 4096 in all
- pair_slots: int32 [16], replicated, may hold values from 0 to 15, each once
- token_logratio: float32 [4096], P('ctx'), may hold values from -0.6 to 0.6
- out_cotangent: bfloat16 [4096, 8192], P('ctx', 'tp'), may hold values from -6 to 6
- attn_cotangent: bfloat16 [4096, 8192], P('ctx', 'tp'), may hold values from -6 to 6
Outputs:
- attention_output_rows: bfloat16 [4096, 8192], P('ctx', 'tp')
- output_adapter_term: bfloat16 [4096, 8192], P('ctx', 'tp')
- input_adapter_gradient: bfloat16 [4096, 8192], P('ctx', 'tp')
- value_down_gradient: float32 [8192, 16], P('tp')
- value_up_gradient: float32 [16, 1024], P(None, 'tp')
- output_down_gradient: float32 [8192, 16], P('tp')
- output_up_gradient: float32 [16, 8192], P(None, 'tp')
The draws below stay inside these ranges and needn't reach their ends.
Inputs may be any that keep to these rules, and one draw needn't show every extreme that they name: `doc_lengths`: the lengths sum to 4096, and the longest document has exactly 1536 tokens. `pair_slots`: each value once; the documents with slots 2p and 2p + 1 answer the same prompt, the even slot being the chosen answer and the odd one the rejected answer.
All inputs are finite; a program needn't handle non-finite values.
Results may differ from the reference program's by a relative error of at most 0.022.
Values may be sent and summed in bfloat16 or wider, within the bound.
A program may use at most 128 MiB of HBM per device.

```python
import math
import jax
import jax.numpy as jnp
import numpy as np
from jax import lax

D = 8192
HEADS = 64
KV_HEADS = 8
HD = 128
RANK = 16
TOK_DEV = 512
TOKENS = 4096
MAXDOC = 1536
NDOCS = 16
N_CTX = 8


def draw_rotated_keys(key, part):
    fresh = jax.random.fold_in(key, 11)
    result = jnp.clip(jax.random.normal(fresh, (TOKENS, KV_HEADS * HD), jnp.float32), -6.0, 6.0)
    return result.astype(jnp.bfloat16)


def draw_queries(key, part):
    fresh = jax.random.fold_in(key, 13)
    result = jnp.clip(jax.random.normal(fresh, (TOKENS, HEADS * HD), jnp.float32), -6.0, 6.0)
    return result.astype(jnp.bfloat16)


def steps_of(own_key, extent, split, low, high):
    gain, own = 1.0, jax.random.fold_in(own_key, 6)
    for dim, blocks in split:
        draws = jnp.exp(jax.random.uniform(jax.random.fold_in(own, dim), (blocks,), jnp.float32, low / len(split), high / len(split)))
        gain = gain * jnp.repeat(draws, extent[dim] // blocks).reshape([-1 if axis == dim else 1 for axis in range(len(extent))])
    return gain


def split_up(count, total, most, lean):
    loads = [(1 << 20) // math.isqrt(grade ** lean) + 1 for grade in range(2, count + 1)]
    surplus, counts = total - most - (count - 1), [1] * (count - 1)
    while surplus > 0:
        movable = [i for i in range(count - 1) if counts[i] < most]
        whole, left = sum([loads[i] for i in movable]), surplus
        for i in movable:
            addition = min(most - counts[i], max(1, left * loads[i] // whole), surplus)
            counts[i] = counts[i] + addition
            surplus = surplus - addition
    return np.array([most] + counts)


def uneven(stream_key, number_of, total, bound, lean):
    if number_of == 2:
        one = jax.random.randint(stream_key, (), max(1, total - bound), min(bound, total - 1) + 1)
        return jnp.stack([one, total - one])
    sizes = jnp.asarray(split_up(number_of, total, bound, lean), jnp.int32)
    pairs = (number_of - 1) // 2
    donor, receiver = sizes[1:1 + 2 * pairs:2], sizes[2:2 + 2 * pairs:2]
    room = jnp.minimum(donor - 1, bound - receiver)
    passed = jax.random.randint(jax.random.fold_in(stream_key, 1), (pairs,), 0, 1 << 20) % (room + 1)
    sizes = sizes.at[1:1 + 2 * pairs:2].set(donor - passed).at[2:2 + 2 * pairs:2].set(receiver + passed)
    return sizes[jax.random.permutation(jax.random.fold_in(stream_key, 2), number_of)]


def gaussian(own_key, extent, width, most, cuts=(), held_as=jnp.bfloat16):
    entries = width * jax.random.normal(own_key, extent, jnp.float32)
    if cuts:
        entries = entries * steps_of(own_key, extent, cuts, -0.22, 0.18)
    return jnp.clip(entries, -most, most).astype(held_as)


def setup_inputs(seed: int = 0) -> dict:
    splits = jax.random.split(jax.random.key(seed), 14)
    hidden = gaussian(splits[0], (TOKENS, D), 1.0, 6.0, ((0, 8), (1, 4)))
    queries = draw_queries(jax.random.fold_in(splits[13], 71), 0)
    rotated_keys = draw_rotated_keys(jax.random.fold_in(splits[13], 71), 0)
    frozen_value_rows = gaussian(splits[3], (TOKENS, KV_HEADS * HD), 1.0, 6.0, ((0, 8), (1, 4)))
    adapter_a_v = gaussian(splits[4], (D, RANK), D ** -0.5, 0.0625, ((0, 4),))
    value_up_matrix = gaussian(splits[5], (RANK, KV_HEADS * HD), RANK ** -0.5, 1.5, ((1, 4),))
    adapter_a_o = gaussian(splits[6], (HEADS * HD, RANK), (HEADS * HD) ** -0.5, 0.0625, ((0, 4),))
    output_up_matrix = gaussian(splits[7], (RANK, D), RANK ** -0.5, 1.5, ((1, 4),))
    doc_lengths = uneven(splits[8], NDOCS, TOKENS, MAXDOC, 2).astype(jnp.int32)
    pair_slots = jax.random.permutation(splits[9], NDOCS).astype(jnp.int32)
    token_logratio = gaussian(splits[10], (TOKENS,), 0.1, 0.6, ((0, 8),), jnp.float32)
    out_cotangent = gaussian(splits[11], (TOKENS, D), 1.0, 6.0, ((0, 8), (1, 4)))
    attn_cotangent = gaussian(splits[12], (TOKENS, HEADS * HD), 1.0, 6.0, ((0, 8), (1, 4)))
    return dict(hidden=hidden, queries=queries, rotated_keys=rotated_keys, frozen_value_rows=frozen_value_rows, adapter_a_v=adapter_a_v, value_up_matrix=value_up_matrix, adapter_a_o=adapter_a_o, output_up_matrix=output_up_matrix, doc_lengths=doc_lengths, pair_slots=pair_slots, token_logratio=token_logratio, out_cotangent=out_cotangent, attn_cotangent=attn_cotangent)


ADAPTER_SCALE = 2.0
BETA = 0.5
NEG_FILL = -1e+30

def doc_index(positions, doc_ends):
    return lax.optimization_barrier(jnp.sum((doc_ends[None, :] <= positions[:, None]).astype(jnp.int32), axis=1))

def doc_weights(margins, pair_slots):
    pair_ids = pair_slots // 2
    signs = jnp.where(pair_slots % 2 == 0, 1.0, -1.0).astype(jnp.float32)
    same_pair = (pair_ids[:, None] == pair_ids[None, :]).astype(jnp.float32)
    gaps = lax.optimization_barrier(jnp.sum(same_pair * (signs * margins)[None, :], axis=1))
    return -BETA * signs * jax.nn.sigmoid(-BETA * gaps)

def reference(hidden, queries, rotated_keys, frozen_value_rows, adapter_a_v, value_up_matrix, adapter_a_o, output_up_matrix, doc_lengths, pair_slots, token_logratio, out_cotangent, attn_cotangent):
    group_size = HEADS // KV_HEADS
    front_pad = 3 * TOK_DEV
    kv_width = KV_HEADS * HD
    score_scale = 1.0 / math.sqrt(HD)
    doc_ends = jnp.cumsum(doc_lengths).astype(jnp.int32)
    positions = jnp.arange(TOKENS, dtype=jnp.int32)
    doc_ids = doc_index(positions, doc_ends)
    onehot = (doc_ids[:, None] == jnp.arange(NDOCS, dtype=jnp.int32)[None, :]).astype(jnp.float32)
    margins = lax.optimization_barrier(jnp.sum(onehot * token_logratio[:, None], axis=0))
    token_weight = lax.optimization_barrier(jnp.sum(onehot * doc_weights(margins, pair_slots)[None, :], axis=1))
    value_down_rows = jnp.dot(hidden, adapter_a_v, preferred_element_type=jnp.float32).astype(jnp.bfloat16)
    value_rows = (frozen_value_rows.astype(jnp.float32) + ADAPTER_SCALE * jnp.dot(value_down_rows, value_up_matrix, preferred_element_type=jnp.float32)).astype(jnp.bfloat16)
    output_gradient_rows = (token_weight[:, None] * out_cotangent.astype(jnp.float32)).astype(jnp.bfloat16)
    output_down_row_gradient = (ADAPTER_SCALE * jnp.dot(output_gradient_rows, output_up_matrix.T, preferred_element_type=jnp.float32)).astype(jnp.bfloat16)
    attn_grad = (token_weight[:, None] * attn_cotangent.astype(jnp.float32) + jnp.dot(output_down_row_gradient, adapter_a_o.T, preferred_element_type=jnp.float32)).astype(jnp.bfloat16)
    padded_keys = jnp.concatenate([jnp.zeros((front_pad, kv_width), jnp.bfloat16), rotated_keys], axis=0)
    padded_values = jnp.concatenate([jnp.zeros((front_pad, kv_width), jnp.bfloat16), value_rows], axis=0)

    def block_step(carried, block_index):
        first_row = (block_index * TOK_DEV).astype(jnp.int32)
        query_pos = first_row + jnp.arange(TOK_DEV, dtype=jnp.int32)
        key_pos = first_row - front_pad + jnp.arange(4 * TOK_DEV, dtype=jnp.int32)
        query_doc = doc_index(query_pos, doc_ends)
        key_doc = doc_index(key_pos, doc_ends)
        allowed = (query_doc[:, None] == key_doc[None, :]) & (key_pos[None, :] <= query_pos[:, None]) & (key_pos[None, :] >= 0)
        query_block = lax.dynamic_slice_in_dim(queries, first_row, TOK_DEV, 0).astype(jnp.float32).reshape(TOK_DEV, KV_HEADS, group_size, HD)
        key_block = lax.dynamic_slice_in_dim(padded_keys, first_row, 4 * TOK_DEV, 0).astype(jnp.float32).reshape(4 * TOK_DEV, KV_HEADS, HD)
        value_block = lax.dynamic_slice_in_dim(padded_values, first_row, 4 * TOK_DEV, 0).astype(jnp.float32).reshape(4 * TOK_DEV, KV_HEADS, HD)
        scores = jnp.einsum('ikgd,jkd->kgij', query_block, key_block) * score_scale
        scores = jnp.where(allowed[None, None], scores, NEG_FILL)
        row_top = lax.optimization_barrier(jnp.max(scores, axis=-1, keepdims=True))
        exponent = jnp.exp(scores - row_top)
        attention = (exponent / lax.optimization_barrier(jnp.sum(exponent, axis=-1, keepdims=True))).astype(jnp.bfloat16)
        output = jnp.einsum('kgij,jkd->ikgd', attention.astype(jnp.float32), value_block).astype(jnp.bfloat16).reshape(TOK_DEV, HEADS * HD)
        grad_block = lax.dynamic_slice_in_dim(attn_grad, first_row, TOK_DEV, 0).astype(jnp.float32).reshape(TOK_DEV, KV_HEADS, group_size, HD)
        term = jnp.einsum('kgij,ikgd->jkd', attention.astype(jnp.float32), grad_block).reshape(4 * TOK_DEV, kv_width)
        current = lax.dynamic_slice_in_dim(carried, first_row, 4 * TOK_DEV, 0)
        carried = lax.dynamic_update_slice_in_dim(carried, current + term, first_row, 0)
        return (carried, output)
    carried, outputs = lax.scan(block_step, jnp.zeros((TOKENS + front_pad, kv_width), jnp.float32), jnp.arange(N_CTX, dtype=jnp.int32))
    attention_output_rows = outputs.reshape(TOKENS, HEADS * HD)
    value_gradient_rows = carried[front_pad:].astype(jnp.bfloat16)
    output_down_rows = jnp.dot(attention_output_rows, adapter_a_o, preferred_element_type=jnp.float32).astype(jnp.bfloat16)
    output_adapter_term = (ADAPTER_SCALE * jnp.dot(output_down_rows, output_up_matrix, preferred_element_type=jnp.float32)).astype(jnp.bfloat16)
    value_down_row_gradient = (ADAPTER_SCALE * jnp.dot(value_gradient_rows, value_up_matrix.T, preferred_element_type=jnp.float32)).astype(jnp.bfloat16)
    input_adapter_gradient = jnp.dot(value_down_row_gradient, adapter_a_v.T, preferred_element_type=jnp.float32).astype(jnp.bfloat16)
    value_down_gradient = jnp.dot(hidden.T, value_down_row_gradient, preferred_element_type=jnp.float32)
    value_up_gradient = ADAPTER_SCALE * jnp.dot(value_down_rows.T, value_gradient_rows, preferred_element_type=jnp.float32)
    output_down_gradient = jnp.dot(attention_output_rows.T, output_down_row_gradient, preferred_element_type=jnp.float32)
    output_up_gradient = ADAPTER_SCALE * jnp.dot(output_down_rows.T, output_gradient_rows, preferred_element_type=jnp.float32)
    return (attention_output_rows, output_adapter_term, input_adapter_gradient, value_down_gradient, value_up_gradient, output_down_gradient, output_up_gradient)
```

```python
import math

import jax
import jax.numpy as jnp
from jax import lax
from jax.experimental import pallas as pl
from jax.experimental.pallas import tpu as pltpu
from jax.sharding import PartitionSpec as P

HEADS = 64
KV_HEADS = 8
HD = 128


ADAPTER_SCALE = 2.0
BETA = 0.5
NEG_FILL = -1e30


def from_behind(value, axis, by):
    peers = lax.axis_size(axis)
    pairs = [(i, i + by) for i in range(peers) if 0 <= i + by < peers]
    return lax.ppermute(value, axis, pairs)


def doc_index(positions, doc_ends):
    return jnp.sum((doc_ends[None, :] <= positions[:, None]).astype(jnp.int32), axis=1)


def doc_weights(margins, pair_slots):
    pair_ids = pair_slots // 2
    signs = jnp.where(pair_slots % 2 == 0, 1.0, -1.0).astype(jnp.float32)
    same_pair = (pair_ids[:, None] == pair_ids[None, :]).astype(jnp.float32)
    gaps = jnp.sum(same_pair * (signs * margins)[None, :], axis=1)
    return -BETA * signs * jax.nn.sigmoid(-BETA * gaps)


def lowrank_sum(local_term):
    return lax.psum(local_term, "tp")


def score_block(left, right):
    return lax.dot_general(
        left, right, (((1,), (1,)), ((), ())), preferred_element_type=jnp.float32
    )


def row_contraction(left, right):
    return lax.dot_general(
        left, right, (((0,), (0,)), ((), ())), preferred_element_type=jnp.float32
    )

TILE = 256
STEP_HEADS = 4
EXP2_SCALE = 1.4426950408889634 / math.sqrt(HD)


def attention_kernel(
    reach_ref,
    query_ref,
    key_ref,
    value_ref,
    cot_ref,
    weight_ref,
    low_grad_ref,
    low_grad_t_ref,
    down_t_ref,
    start_ref,
    out_ref,
    value_grad_ref,
    low_out_ref,
    down_grad_ref,
    bias,
    scores,
    weights,
    value_t,
    value_acc,
):
    step = pl.program_id(0)
    steps_per_kv = HEADS // KV_HEADS // STEP_HEADS
    row_count = query_ref.shape[0]
    window = key_ref.shape[0]
    tiles = window // TILE
    query_tiles = row_count // TILE

    @pl.when(step == 0)
    def _():
        low_out_ref[...] = jnp.zeros_like(low_out_ref)

        @pl.loop(0, query_tiles)
        def _(qt):
            first = reach_ref[2 * qt]
            lane = pl.ds(pl.multiple_of(qt * TILE, TILE), TILE)
            starts = start_ref[:, lane]
            query_pos = (
                window - row_count + qt * TILE + lax.broadcasted_iota(jnp.int32, (1, TILE), 1)
            )

            @pl.loop(0, reach_ref[2 * qt + 1])
            def _(k):
                key_pos = (first + k) * TILE + lax.broadcasted_iota(
                    jnp.int32, (TILE, TILE), 0
                )
                allowed = (key_pos >= starts) & (key_pos <= query_pos)
                rows = pl.ds(pl.multiple_of(k * TILE, TILE), TILE)
                bias[qt, rows, :] = jnp.where(allowed, 0.0, NEG_FILL)

    @pl.when(step % steps_per_kv == 0)
    def _():
        value_acc[...] = jnp.zeros_like(value_acc)
        for k in range(tiles):
            rows = slice(k * TILE, (k + 1) * TILE)
            value_t[:, rows] = jnp.transpose(value_ref[rows, :].astype(jnp.float32)).astype(
                jnp.bfloat16
            )

    def one_head(qt, first, count, h):
        rows = pl.ds(pl.multiple_of(qt * TILE, TILE), TILE)
        columns = pl.ds(pl.multiple_of(h * HD, HD), HD)
        query = query_ref[rows, columns]

        def key_rows(k):
            return pl.ds(pl.multiple_of((first + k) * TILE, TILE), TILE)

        top = jnp.full((8, TILE), NEG_FILL, jnp.float32)
        for k in range(count):
            span = slice(k * TILE, (k + 1) * TILE)
            block = score_block(key_ref[key_rows(k), :], query) + bias[qt, span, :]
            scores[span, :] = block
            top = jnp.maximum(top, jnp.max(block.reshape(TILE // 8, 8, TILE), axis=0))
        top = jnp.max(top, axis=0, keepdims=True) * EXP2_SCALE
        total = jnp.zeros((8, TILE), jnp.float32)
        output = jnp.zeros((HD, TILE), jnp.float32)
        for k in range(count):
            span = slice(k * TILE, (k + 1) * TILE)
            block = jnp.exp2(scores[span, :] * EXP2_SCALE - top)
            total = total + jnp.sum(block.reshape(TILE // 8, 8, TILE), axis=0)
            block = block.astype(jnp.bfloat16)
            weights[span, :] = block
            output = output + jnp.dot(
                value_t[:, key_rows(k)], block, preferred_element_type=jnp.float32
            )
        inverse = 1.0 / jnp.sum(total, axis=0, keepdims=True)
        out_ref[rows, columns] = jnp.transpose(output * inverse).astype(jnp.bfloat16)
        inverse_rows = jnp.transpose(jnp.broadcast_to(inverse, (HD, TILE)))
        grad = weight_ref[rows, :] * cot_ref[rows, columns].astype(jnp.float32) + jnp.dot(
            low_grad_ref[rows, :], down_t_ref[:, columns], preferred_element_type=jnp.float32
        )
        grad = (grad * inverse_rows).astype(jnp.bfloat16)
        for k in range(count):
            span = slice(k * TILE, (k + 1) * TILE)
            value_acc[key_rows(k), :] += jnp.dot(
                weights[span, :], grad, preferred_element_type=jnp.float32
            )

    @pl.loop(0, query_tiles)
    def _(qt):
        first = reach_ref[2 * qt]
        count = reach_ref[2 * qt + 1]
        for variant in range(1, tiles + 1):

            @pl.when(count == variant)
            def _():
                @pl.loop(0, STEP_HEADS)
                def _(h):
                    one_head(qt, first, variant, h)

    low_out_ref[...] += lax.dot_general(
        down_t_ref[...],
        out_ref[...],
        (((1,), (1,)), ((), ())),
        preferred_element_type=jnp.float32,
    )
    down_grad_ref[...] = jnp.dot(
        low_grad_t_ref[...], out_ref[...], preferred_element_type=jnp.float32
    )

    @pl.when(step % steps_per_kv == steps_per_kv - 1)
    def _():
        value_grad_ref[...] = value_acc[...].astype(value_grad_ref.dtype)


def attention(reach, queries, keys, values, cot, weight, low_grad, down_t, starts):
    row_count, width = queries.shape
    window = keys.shape[0]
    rank = low_grad.shape[1]
    block = STEP_HEADS * HD
    steps = width // block
    steps_per_kv = HEADS // KV_HEADS // STEP_HEADS
    by_step = lambda i, reach: (0, i)
    by_kv = lambda i, reach: (0, i // steps_per_kv)
    whole = lambda i, reach: (0, 0)
    return pl.pallas_call(
        attention_kernel,
        grid_spec=pltpu.PrefetchScalarGridSpec(
            num_scalar_prefetch=1,
            grid=(steps,),
            in_specs=[
                pl.BlockSpec((row_count, block), by_step),
                pl.BlockSpec((window, HD), by_kv),
                pl.BlockSpec((window, HD), by_kv),
                pl.BlockSpec((row_count, block), by_step),
                pl.BlockSpec((row_count, 1), whole),
                pl.BlockSpec((row_count, rank), whole),
                pl.BlockSpec((rank, row_count), whole),
                pl.BlockSpec((rank, block), by_step),
                pl.BlockSpec((1, row_count), whole),
            ],
            out_specs=[
                pl.BlockSpec((row_count, block), by_step),
                pl.BlockSpec((window, HD), by_kv),
                pl.BlockSpec((rank, row_count), whole),
                pl.BlockSpec((rank, block), by_step),
            ],
            scratch_shapes=[
                pltpu.VMEM((row_count // TILE, window, TILE), jnp.float32),
                pltpu.VMEM((window, TILE), jnp.float32),
                pltpu.VMEM((window, TILE), jnp.bfloat16),
                pltpu.VMEM((HD, window), jnp.bfloat16),
                pltpu.VMEM((window, HD), jnp.float32),
            ],
        ),
        out_shape=[
            jax.ShapeDtypeStruct((row_count, width), jnp.bfloat16),
            jax.ShapeDtypeStruct(keys.shape, jnp.bfloat16),
            jax.ShapeDtypeStruct((rank, row_count), jnp.float32),
            jax.ShapeDtypeStruct((rank, width), jnp.float32),
        ],
        compiler_params=pltpu.CompilerParams(vmem_limit_bytes=40 * 1024 * 1024),
    )(reach, queries, keys, values, cot, weight, low_grad, low_grad.T, down_t, starts)


def tile_reach(first_row, row_count, doc_ends):
    query_pos = first_row + jnp.arange(row_count, dtype=jnp.int32)
    ended = doc_ends[None, :] <= query_pos[:, None]
    starts = jnp.max(jnp.where(ended, doc_ends[None, :], 0), axis=1)
    starts = starts - (first_row - 3 * row_count)
    firsts = starts[::TILE] // TILE
    lasts = (3 * row_count) // TILE + jnp.arange(row_count // TILE, dtype=jnp.int32)
    reach = jnp.stack([firsts, lasts - firsts + 1], axis=1).reshape(-1)
    return reach.astype(jnp.int32), starts.astype(jnp.int32)[None, :]


def shards(
    hidden,
    queries,
    rotated_keys,
    frozen_value_rows,
    adapter_a_v,
    value_up_matrix,
    adapter_a_o,
    output_up_matrix,
    doc_lengths,
    pair_slots,
    token_logratio,
    out_cotangent,
    attn_cotangent,
):
    row_count = hidden.shape[0]
    doc_count = doc_lengths.shape[0]
    first_row = lax.axis_index("ctx") * row_count
    doc_ends = jnp.cumsum(doc_lengths)
    query_pos = first_row + jnp.arange(row_count, dtype=jnp.int32)
    query_doc = doc_index(query_pos, doc_ends)
    reach, starts = tile_reach(first_row, row_count, doc_ends)
    value_down_rows = lowrank_sum(
        jnp.dot(hidden, adapter_a_v, preferred_element_type=jnp.float32)
    ).astype(jnp.bfloat16)
    value_rows = (
        frozen_value_rows.astype(jnp.float32)
        + ADAPTER_SCALE
        * jnp.dot(value_down_rows, value_up_matrix, preferred_element_type=jnp.float32)
    ).astype(jnp.bfloat16)
    own_pair = jnp.stack([rotated_keys, value_rows])
    pieces = [own_pair]
    current = own_pair
    for step_index in range(3):
        current = from_behind(current, "ctx", 1)
        pieces.append(current)
    window = jnp.concatenate(pieces[::-1], axis=1)
    onehot = (query_doc[:, None] == jnp.arange(doc_count, dtype=jnp.int32)[None, :]).astype(
        jnp.float32
    )
    margins = lax.psum(jnp.sum(onehot * token_logratio[:, None], axis=0), "ctx")
    token_weight = jnp.sum(onehot * doc_weights(margins, pair_slots)[None, :], axis=1)
    output_gradient_rows = (token_weight[:, None] * out_cotangent.astype(jnp.float32)).astype(
        jnp.bfloat16
    )
    output_down_row_gradient = (
        ADAPTER_SCALE
        * lowrank_sum(
            jnp.dot(output_gradient_rows, output_up_matrix.T, preferred_element_type=jnp.float32)
        )
    ).astype(jnp.bfloat16)
    attention_output_rows, value_window, low_out_t, down_grad_t = attention(
        reach,
        queries,
        window[0],
        window[1],
        attn_cotangent,
        token_weight[:, None],
        output_down_row_gradient,
        adapter_a_o.T,
        starts,
    )
    slot_terms = [
        value_window[slot_index * row_count : (slot_index + 1) * row_count]
        for slot_index in range(4)
    ]
    carried = slot_terms[0]
    for step_index in range(1, 4):
        carried = from_behind(carried, "ctx", -1) + slot_terms[step_index]
    value_gradient_rows = carried.astype(jnp.bfloat16)
    output_down_rows = lowrank_sum(low_out_t).T.astype(jnp.bfloat16)
    output_adapter_term = (
        ADAPTER_SCALE
        * jnp.dot(output_down_rows, output_up_matrix, preferred_element_type=jnp.float32)
    ).astype(jnp.bfloat16)
    value_down_row_gradient = (
        ADAPTER_SCALE
        * lowrank_sum(
            jnp.dot(value_gradient_rows, value_up_matrix.T, preferred_element_type=jnp.float32)
        )
    ).astype(jnp.bfloat16)
    input_adapter_gradient = jnp.dot(
        value_down_row_gradient, adapter_a_v.T, preferred_element_type=jnp.float32
    ).astype(jnp.bfloat16)
    local_a_v = row_contraction(hidden, value_down_row_gradient)
    local_value_up = ADAPTER_SCALE * row_contraction(value_down_rows, value_gradient_rows)
    local_a_o = down_grad_t.T
    local_output_up = ADAPTER_SCALE * row_contraction(output_down_rows, output_gradient_rows)
    value_down_gradient, value_up_gradient, output_down_gradient, output_up_gradient = (
        lax.psum(local_a_v.astype(jnp.bfloat16), "ctx").astype(jnp.float32),
        lax.psum(local_value_up.astype(jnp.bfloat16), "ctx").astype(jnp.float32),
        lax.psum(local_a_o.astype(jnp.bfloat16), "ctx").astype(jnp.float32),
        lax.psum(local_output_up.astype(jnp.bfloat16), "ctx").astype(jnp.float32),
    )
    return (
        attention_output_rows,
        output_adapter_term,
        input_adapter_gradient,
        value_down_gradient,
        value_up_gradient,
        output_down_gradient,
        output_up_gradient,
    )


def solution(mesh):
    in_specs = (
        P("ctx", "tp"),
        P("ctx", "tp"),
        P("ctx", "tp"),
        P("ctx", "tp"),
        P("tp", None),
        P(None, "tp"),
        P("tp", None),
        P(None, "tp"),
        P(),
        P(),
        P("ctx"),
        P("ctx", "tp"),
        P("ctx", "tp"),
    )
    out_specs = (
        P("ctx", "tp"),
        P("ctx", "tp"),
        P("ctx", "tp"),
        P("tp", None),
        P(None, "tp"),
        P("tp", None),
        P(None, "tp"),
    )
    return jax.shard_map(shards, mesh=mesh, in_specs=in_specs, out_specs=out_specs, check_vma=False)
```

```python
import math

import jax
import jax.numpy as jnp
from jax import lax
from jax.experimental import pallas as pl
from jax.experimental.pallas import tpu as pltpu
from jax.sharding import PartitionSpec as P

HEADS = 64
KV_HEADS = 8
HD = 128


ADAPTER_SCALE = 2.0
BETA = 0.5
NEG_FILL = -1e30


def doc_index(positions, doc_ends):
    return jnp.sum((doc_ends[None, :] <= positions[:, None]).astype(jnp.int32), axis=1)


def doc_weights(margins, pair_slots):
    pair_ids = pair_slots // 2
    signs = jnp.where(pair_slots % 2 == 0, 1.0, -1.0).astype(jnp.float32)
    same_pair = (pair_ids[:, None] == pair_ids[None, :]).astype(jnp.float32)
    gaps = jnp.sum(same_pair * (signs * margins)[None, :], axis=1)
    return -BETA * signs * jax.nn.sigmoid(-BETA * gaps)


def score_block(left, right):
    return lax.dot_general(
        left, right, (((1,), (1,)), ((), ())), preferred_element_type=jnp.float32
    )


def row_contraction(left, right):
    return lax.dot_general(
        left, right, (((0,), (0,)), ((), ())), preferred_element_type=jnp.float32
    )

TILE = 256
STEP_HEADS = 4
EXP2_SCALE = 1.4426950408889634 / math.sqrt(HD)


def attention_kernel(
    reach_ref,
    query_ref,
    key_ref,
    value_ref,
    cot_ref,
    weight_ref,
    low_grad_t_ref,
    down_t_ref,
    start_ref,
    out_ref,
    value_grad_ref,
    low_out_ref,
    down_grad_ref,
    bias,
    scores,
    weights,
    value_t,
    value_acc,
):
    step = pl.program_id(0)
    steps_per_kv = HEADS // KV_HEADS // STEP_HEADS
    row_count = query_ref.shape[0]
    window = key_ref.shape[0]
    tiles = window // TILE
    query_tiles = row_count // TILE

    @pl.when(step == 0)
    def _():
        low_out_ref[...] = jnp.zeros_like(low_out_ref)

        @pl.loop(0, query_tiles)
        def _(qt):
            first = reach_ref[2 * qt]
            lane = pl.ds(pl.multiple_of(qt * TILE, TILE), TILE)
            starts = start_ref[:, lane]
            query_pos = (
                window - row_count + qt * TILE + lax.broadcasted_iota(jnp.int32, (1, TILE), 1)
            )

            @pl.loop(0, reach_ref[2 * qt + 1])
            def _(k):
                key_pos = (first + k) * TILE + lax.broadcasted_iota(
                    jnp.int32, (TILE, TILE), 0
                )
                allowed = (key_pos >= starts) & (key_pos <= query_pos)
                rows = pl.ds(pl.multiple_of(k * TILE, TILE), TILE)
                bias[qt, rows, :] = jnp.where(allowed, 0.0, NEG_FILL)

    @pl.when(step % steps_per_kv == 0)
    def _():
        value_acc[...] = jnp.zeros_like(value_acc)
        for k in range(tiles):
            rows = slice(k * TILE, (k + 1) * TILE)
            value_t[:, rows] = jnp.transpose(value_ref[rows, :].astype(jnp.float32)).astype(
                jnp.bfloat16
            )

    def one_head(qt, first, count, h):
        rows = pl.ds(pl.multiple_of(qt * TILE, TILE), TILE)
        columns = pl.ds(pl.multiple_of(h * HD, HD), HD)
        query = query_ref[rows, columns]

        def key_rows(k):
            return pl.ds(pl.multiple_of((first + k) * TILE, TILE), TILE)

        top = jnp.full((8, TILE), NEG_FILL, jnp.float32)
        for k in range(count):
            span = slice(k * TILE, (k + 1) * TILE)
            block = score_block(key_ref[key_rows(k), :], query) + bias[qt, span, :]
            scores[span, :] = block
            top = jnp.maximum(top, jnp.max(block.reshape(TILE // 8, 8, TILE), axis=0))
        top = jnp.max(top, axis=0, keepdims=True) * EXP2_SCALE
        total = jnp.zeros((8, TILE), jnp.float32)
        output = jnp.zeros((HD, TILE), jnp.float32)
        for k in range(count):
            span = slice(k * TILE, (k + 1) * TILE)
            block = jnp.exp2(scores[span, :] * EXP2_SCALE - top)
            total = total + jnp.sum(block.reshape(TILE // 8, 8, TILE), axis=0)
            block = block.astype(jnp.bfloat16)
            weights[span, :] = block
            output = output + jnp.dot(
                value_t[:, key_rows(k)], block, preferred_element_type=jnp.float32
            )
        inverse = 1.0 / jnp.sum(total, axis=0, keepdims=True)
        out_ref[rows, columns] = jnp.transpose(output * inverse).astype(jnp.bfloat16)
        inverse_rows = jnp.transpose(jnp.broadcast_to(inverse, (HD, TILE)))
        grad = weight_ref[rows, :] * cot_ref[rows, columns].astype(jnp.float32) + row_contraction(
            low_grad_t_ref[:, rows], down_t_ref[:, columns]
        )
        grad = (grad * inverse_rows).astype(jnp.bfloat16)
        for k in range(count):
            span = slice(k * TILE, (k + 1) * TILE)
            value_acc[key_rows(k), :] += jnp.dot(
                weights[span, :], grad, preferred_element_type=jnp.float32
            )

    @pl.loop(0, query_tiles)
    def _(qt):
        first = reach_ref[2 * qt]
        count = reach_ref[2 * qt + 1]
        for variant in range(1, tiles + 1):

            @pl.when(count == variant)
            def _():
                @pl.loop(0, STEP_HEADS)
                def _(h):
                    one_head(qt, first, variant, h)

    low_out_ref[...] += lax.dot_general(
        down_t_ref[...],
        out_ref[...],
        (((1,), (1,)), ((), ())),
        preferred_element_type=jnp.float32,
    )
    down_grad_ref[...] = jnp.dot(
        low_grad_t_ref[...], out_ref[...], preferred_element_type=jnp.float32
    )

    @pl.when(step % steps_per_kv == steps_per_kv - 1)
    def _():
        value_grad_ref[...] = value_acc[...].astype(value_grad_ref.dtype)


def attention(reach, queries, keys, values, cot, weight, low_grad_t, down_t, starts):
    row_count, width = queries.shape
    window = keys.shape[0]
    rank = low_grad_t.shape[0]
    block = STEP_HEADS * HD
    steps = width // block
    steps_per_kv = HEADS // KV_HEADS // STEP_HEADS
    by_step = lambda i, reach: (0, i)
    by_kv = lambda i, reach: (0, i // steps_per_kv)
    whole = lambda i, reach: (0, 0)
    return pl.pallas_call(
        attention_kernel,
        grid_spec=pltpu.PrefetchScalarGridSpec(
            num_scalar_prefetch=1,
            grid=(steps,),
            in_specs=[
                pl.BlockSpec((row_count, block), by_step),
                pl.BlockSpec((window, HD), by_kv),
                pl.BlockSpec((window, HD), by_kv),
                pl.BlockSpec((row_count, block), by_step),
                pl.BlockSpec((row_count, 1), whole),
                pl.BlockSpec((rank, row_count), whole),
                pl.BlockSpec((rank, block), by_step),
                pl.BlockSpec((1, row_count), whole),
            ],
            out_specs=[
                pl.BlockSpec((row_count, block), by_step),
                pl.BlockSpec((window, HD), by_kv),
                pl.BlockSpec((rank, row_count), whole),
                pl.BlockSpec((rank, block), by_step),
            ],
            scratch_shapes=[
                pltpu.VMEM((row_count // TILE, window, TILE), jnp.float32),
                pltpu.VMEM((window, TILE), jnp.float32),
                pltpu.VMEM((window, TILE), jnp.bfloat16),
                pltpu.VMEM((HD, window), jnp.bfloat16),
                pltpu.VMEM((window, HD), jnp.float32),
            ],
        ),
        out_shape=[
            jax.ShapeDtypeStruct((row_count, width), jnp.bfloat16),
            jax.ShapeDtypeStruct(keys.shape, jnp.bfloat16),
            jax.ShapeDtypeStruct((rank, row_count), jnp.float32),
            jax.ShapeDtypeStruct((rank, width), jnp.float32),
        ],
        compiler_params=pltpu.CompilerParams(vmem_limit_bytes=40 * 1024 * 1024),
    )(reach, queries, keys, values, cot, weight, low_grad_t, down_t, starts)


def tile_reach(first_row, row_count, doc_ends):
    query_pos = first_row + jnp.arange(row_count, dtype=jnp.int32)
    ended = doc_ends[None, :] <= query_pos[:, None]
    starts = jnp.max(jnp.where(ended, doc_ends[None, :], 0), axis=1)
    starts = starts - (first_row - 3 * row_count)
    firsts = starts[::TILE] // TILE
    lasts = (3 * row_count) // TILE + jnp.arange(row_count // TILE, dtype=jnp.int32)
    reach = jnp.stack([firsts, lasts - firsts + 1], axis=1).reshape(-1)
    return reach.astype(jnp.int32), starts.astype(jnp.int32)[None, :]

MESH = pl.DeviceIdType.MESH


def greet_all():
    barrier = pltpu.get_barrier_semaphore()
    count = 0
    for axis in ("ctx", "tp"):
        size = lax.axis_size(axis)
        place = lax.axis_index(axis)
        for hop in range(1, size):
            pl.semaphore_signal(
                barrier, inc=1, device_id={axis: (place + hop) % size}, device_id_type=MESH
            )
            count += 1
    pl.semaphore_wait(barrier, count)


def send_to(axis, place, source, target, send_sem, recv_sem):
    return pltpu.make_async_remote_copy(
        src_ref=source,
        dst_ref=target,
        send_sem=send_sem,
        recv_sem=recv_sem,
        device_id={axis: place},
        device_id_type=MESH,
    )


def send_round(axis, source, slots, send_sems, recv_sems):
    size = lax.axis_size(axis)
    place = lax.axis_index(axis)
    copies = []
    for hop in range(1, size):
        copy = send_to(
            axis,
            (place + hop) % size,
            source((place + hop) % size),
            slots(hop),
            send_sems.at[hop - 1],
            recv_sems.at[hop - 1],
        )
        copy.start()
        copies.append(copy)
    return copies


def slot_total(own, copies, slots):
    total = own.astype(jnp.float32)
    for hop, copy in enumerate(copies):
        copy.wait_recv()
        total = total + slots[hop].astype(jnp.float32)
    return total


def begin_kernel(
    hidden_ref,
    down_v_t_ref,
    cot_ref,
    up_ref,
    key_ref,
    frozen_ref,
    value_up_ref,
    ratio_ref,
    begins_ref,
    ends_ref,
    key_win_ref,
    value_win_ref,
    low_v_ref,
    low_grad_ref,
    margin_ref,
    pack,
    pack_slots,
    margin_own,
    margin_slots,
    frozen_slots,
    low_slots,
    pack_send,
    pack_recv,
    margin_send,
    margin_recv,
    rows_send,
    rows_recv,
    low_send,
    low_recv,
):
    ctx_size = lax.axis_size("ctx")
    place = lax.axis_index("ctx")
    row_count = hidden_ref.shape[0]
    rank = down_v_t_ref.shape[0]
    odd = place % 2
    greet_all()

    def window_rows(slot):
        return pl.ds(pl.multiple_of(slot * row_count, row_count), row_count)

    def row_copies(sources, peer, slot, sem):
        targets = (key_win_ref.at[window_rows(slot), :], frozen_slots.at[slot])
        return [
            send_to(
                "ctx",
                jnp.minimum(peer, ctx_size - 1),
                sources[which],
                targets[which],
                rows_send.at[sem, which],
                rows_recv.at[slot, which],
            )
            for which in range(2)
        ]

    own = (key_ref, frozen_ref)
    near = row_copies(own, place + 1, 2, 0)
    far = row_copies(own, place + 2 + odd, 1 - odd, 1)
    near_on = place + 1 < ctx_size
    far_on = place + 2 + odd < ctx_size

    def passed_on(slot):
        sources = (key_win_ref.at[window_rows(slot), :], frozen_slots.at[slot])
        return row_copies(sources, place + 1, slot - 1, 1 + slot)

    def pass_on(slot):
        return (odd == 0) & near_on & (place >= 3 - slot)

    @pl.when(far_on)
    def _():
        for copy in far:
            copy.start()

    @pl.when(near_on)
    def _():
        for copy in near:
            copy.start()

    for slot in range(3):

        @pl.when(place < 3 - slot)
        def _():
            key_win_ref[slot * row_count : (slot + 1) * row_count, :] = jnp.zeros(
                key_ref.shape, key_ref.dtype
            )
            frozen_slots[slot] = jnp.zeros(frozen_ref.shape, frozen_ref.dtype)
            low_slots[slot] = jnp.zeros(low_v_ref.shape, low_v_ref.dtype)

    positions = place * row_count + lax.broadcasted_iota(
        jnp.int32, (begins_ref.shape[0], row_count), 1
    )
    member = (positions >= begins_ref[...]) & (positions < ends_ref[...])
    margins = jnp.sum(jnp.where(member, ratio_ref[...], 0.0), axis=1, keepdims=True)
    margin_own[...] = jnp.broadcast_to(margins, margin_own.shape)
    margin_copies = send_round(
        "ctx", lambda peer: margin_own, lambda hop: margin_slots.at[hop - 1], margin_send, margin_recv
    )
    pack[0:rank, :] = score_block(down_v_t_ref[...], hidden_ref[...])
    pack[rank : 2 * rank, :] = score_block(up_ref[...], cot_ref[...])
    pack_copies = send_round(
        "tp", lambda peer: pack, lambda hop: pack_slots.at[hop - 1], pack_send, pack_recv
    )
    key_win_ref[3 * row_count : 4 * row_count, :] = key_ref[...]
    sums = slot_total(pack[...], pack_copies, pack_slots)
    low_v_ref[...] = sums[0:rank, :].astype(jnp.bfloat16)
    low_grad_ref[...] = sums[rank : 2 * rank, :]
    low_copies = [
        send_to(
            "ctx",
            jnp.minimum(place + hop, ctx_size - 1),
            low_v_ref,
            low_slots.at[3 - hop],
            low_send.at[hop - 1],
            low_recv.at[hop - 1],
        )
        for hop in range(1, 4)
    ]
    for hop in range(1, 4):

        @pl.when(place + hop < ctx_size)
        def _():
            low_copies[hop - 1].start()

    for slot in (2, 1):

        @pl.when(pass_on(slot))
        def _():
            for which in range(2):
                row_copies(own, place + 1, slot, 0)[which].wait_recv()
            for copy in passed_on(slot):
                copy.start()

    margin_ref[...] = slot_total(margin_own[...], margin_copies, margin_slots)

    def rows_of(low, frozen):
        return (
            frozen.astype(jnp.float32) + ADAPTER_SCALE * row_contraction(low, value_up_ref[...])
        ).astype(jnp.bfloat16)

    value_win_ref[3 * row_count : 4 * row_count, :] = rows_of(low_v_ref[...], frozen_ref[...])
    for slot in (2, 1, 0):

        @pl.when(place >= 3 - slot)
        def _():
            low_copies[2 - slot].wait_recv()

        already = pass_on(slot) if slot > 0 else place < 0

        @pl.when((place >= 3 - slot) & jnp.logical_not(already))
        def _():
            for which in range(2):
                row_copies(own, place + 1, slot, 0)[which].wait_recv()

        value_win_ref[slot * row_count : (slot + 1) * row_count, :] = rows_of(
            low_slots[slot], frozen_slots[slot]
        )

    @pl.when(far_on)
    def _():
        for copy in far:
            copy.wait_send()

    @pl.when(near_on)
    def _():
        for copy in near:
            copy.wait_send()

    for slot in (2, 1):

        @pl.when(pass_on(slot))
        def _():
            for copy in passed_on(slot):
                copy.wait_send()

    for hop in range(1, 4):

        @pl.when(place + hop < ctx_size)
        def _():
            low_copies[hop - 1].wait_send()

    for copy in margin_copies + pack_copies:
        copy.wait_send()


def dma_sems(*shape):
    return pltpu.SemaphoreType.DMA(shape)


def begin(hidden, down_v_t, cot, up, keys, frozen, value_up, ratio, begins, ends):
    row_count = hidden.shape[0]
    rank = up.shape[0]
    docs = begins.shape[0]
    ctx_size, tp_size = lax.axis_size("ctx"), lax.axis_size("tp")
    window = (4 * row_count, keys.shape[1])
    whole = pl.BlockSpec(memory_space=pltpu.VMEM)
    f32, bf16 = jnp.float32, jnp.bfloat16
    return pl.pallas_call(
        begin_kernel,
        in_specs=[whole] * 10,
        out_specs=[whole] * 5,
        out_shape=[
            jax.ShapeDtypeStruct(window, bf16),
            jax.ShapeDtypeStruct(window, bf16),
            jax.ShapeDtypeStruct((rank, row_count), bf16),
            jax.ShapeDtypeStruct((rank, row_count), f32),
            jax.ShapeDtypeStruct((docs, 128), f32),
        ],
        scratch_shapes=[
            pltpu.VMEM((2 * rank, row_count), f32),
            pltpu.VMEM((tp_size - 1, 2 * rank, row_count), f32),
            pltpu.VMEM((docs, 128), f32),
            pltpu.VMEM((ctx_size - 1, docs, 128), f32),
            pltpu.VMEM((3, row_count, keys.shape[1]), bf16),
            pltpu.VMEM((3, rank, row_count), bf16),
            dma_sems(tp_size - 1),
            dma_sems(tp_size - 1),
            dma_sems(ctx_size - 1),
            dma_sems(ctx_size - 1),
            dma_sems(4, 2),
            dma_sems(3, 2),
            dma_sems(3),
            dma_sems(3),
        ],
        compiler_params=pltpu.CompilerParams(
            collective_id=0, has_side_effects=True, vmem_limit_bytes=40 * 1024 * 1024
        ),
    )(hidden, down_v_t, cot, up, keys, frozen, value_up, ratio, begins, ends)


def finish_kernel(
    value_win_ref,
    low_out_ref,
    hidden_ref,
    cot_ref,
    value_up_ref,
    low_v_ref,
    weight_ref,
    down_grad_ref,
    low_o_ref,
    low_v_grad_ref,
    value_down_ref,
    value_up_grad_ref,
    output_down_ref,
    output_up_ref,
    value_slots,
    low_out_slots,
    low_grad_own,
    low_grad_slots,
    first_own,
    first_slots,
    first_part,
    first_sum,
    second_own,
    second_slots,
    second_part,
    second_sum,
    value_send,
    value_recv,
    low_out_send,
    low_out_recv,
    low_grad_send,
    low_grad_recv,
    first_send,
    first_recv,
    first_back_send,
    first_back_recv,
    second_send,
    second_recv,
    second_back_send,
    second_back_recv,
):
    ctx_size = lax.axis_size("ctx")
    place = lax.axis_index("ctx")
    row_count, width = hidden_ref.shape
    kv_width = value_win_ref.shape[1]
    greet_all()
    low_out_copies = send_round(
        "tp",
        lambda peer: low_out_ref,
        lambda hop: low_out_slots.at[hop - 1],
        low_out_send,
        low_out_recv,
    )
    value_copies = [
        send_to(
            "ctx",
            jnp.maximum(place - hop, 0),
            value_win_ref.at[(3 - hop) * row_count : (4 - hop) * row_count, :],
            value_slots.at[hop - 1],
            value_send.at[hop - 1],
            value_recv.at[hop - 1],
        )
        for hop in range(1, 4)
    ]
    for hop in (3, 2, 1):

        @pl.when(place >= hop)
        def _():
            value_copies[hop - 1].start()

    for hop in range(1, 4):

        @pl.when(place + hop >= ctx_size)
        def _():
            value_slots[hop - 1] = jnp.zeros(value_slots.shape[1:], value_slots.dtype)

    def columns(own, part):
        share = own.shape[1] // ctx_size
        return pl.ds(pl.multiple_of(part * share, 128), share)

    def scatter(own, slots, sends, recvs):
        return send_round(
            "ctx",
            lambda peer: own.at[:, columns(own, peer)],
            lambda hop: slots.at[hop - 1],
            sends,
            recvs,
        )

    def gather(own, copies, slots, part, total, sends, recvs):
        mine = columns(own, place)
        part[...] = slot_total(own[:, mine], copies, slots).astype(jnp.bfloat16)
        total[:, mine] = part[...]
        return send_round(
            "ctx", lambda peer: part, lambda hop: total.at[:, mine], sends, recvs
        )

    def gathered(copies, total, recvs):
        for hop, copy in enumerate(copies):
            peer = (place + ctx_size - hop - 1) % ctx_size
            send_to(
                "ctx", (place + 1) % ctx_size, total.at[:, columns(total, peer)],
                total.at[:, columns(total, peer)], recvs.at[hop], recvs.at[hop],
            ).wait_recv()

    if first_own.shape[1] > 2 * width:
        first_own[:, 2 * width :] = jnp.zeros(
            (first_own.shape[0], first_own.shape[1] - 2 * width), jnp.bfloat16
        )
    if second_own.shape[1] > width + kv_width:
        second_own[:, width + kv_width :] = jnp.zeros(
            (second_own.shape[0], second_own.shape[1] - width - kv_width), jnp.bfloat16
        )
    first_own[:, 0:width] = down_grad_ref[...].astype(jnp.bfloat16)
    low_o = slot_total(low_out_ref[...], low_out_copies, low_out_slots).astype(jnp.bfloat16)
    low_o_ref[...] = low_o
    weighted = (ADAPTER_SCALE * weight_ref[...] * low_o.astype(jnp.float32)).astype(jnp.bfloat16)
    first_own[:, width : 2 * width] = jnp.dot(
        weighted, cot_ref[...], preferred_element_type=jnp.float32
    ).astype(jnp.bfloat16)
    first_copies = scatter(first_own, first_slots, first_send, first_recv)
    total = value_win_ref[3 * row_count : 4 * row_count, :].astype(jnp.float32)
    for hop in range(1, 4):

        @pl.when(place + hop < ctx_size)
        def _():
            value_copies[hop - 1].wait_recv()

        total = total + value_slots[hop - 1].astype(jnp.float32)
    value_grad = total.astype(jnp.bfloat16)
    low_grad_own[...] = ADAPTER_SCALE * score_block(value_up_ref[...], value_grad)
    low_grad_copies = send_round(
        "tp",
        lambda peer: low_grad_own,
        lambda hop: low_grad_slots.at[hop - 1],
        low_grad_send,
        low_grad_recv,
    )
    second_own[:, width : width + kv_width] = (
        ADAPTER_SCALE * jnp.dot(low_v_ref[...], value_grad, preferred_element_type=jnp.float32)
    ).astype(jnp.bfloat16)
    first_back = gather(
        first_own, first_copies, first_slots, first_part, first_sum, first_back_send, first_back_recv
    )
    low_grad = slot_total(low_grad_own[...], low_grad_copies, low_grad_slots).astype(jnp.bfloat16)
    low_v_grad_ref[...] = low_grad
    second_own[:, 0:width] = jnp.dot(
        low_grad, hidden_ref[...], preferred_element_type=jnp.float32
    ).astype(jnp.bfloat16)
    second_copies = scatter(second_own, second_slots, second_send, second_recv)
    gathered(first_back, first_sum, first_back_recv)
    output_down_ref[...] = first_sum[:, 0:width].astype(jnp.float32)
    output_up_ref[...] = first_sum[:, width : 2 * width].astype(jnp.float32)
    second_back = gather(
        second_own,
        second_copies,
        second_slots,
        second_part,
        second_sum,
        second_back_send,
        second_back_recv,
    )
    gathered(second_back, second_sum, second_back_recv)
    value_down_ref[...] = second_sum[:, 0:width].astype(jnp.float32)
    value_up_grad_ref[...] = second_sum[:, width : width + kv_width].astype(jnp.float32)
    for hop in range(1, 4):

        @pl.when(place >= hop)
        def _():
            value_copies[hop - 1].wait_send()

    for copies in (
        low_out_copies,
        low_grad_copies,
        first_copies,
        first_back,
        second_copies,
        second_back,
    ):
        for copy in copies:
            copy.wait_send()


def finish(value_win, low_out, hidden, cot, value_up, low_v, weight, down_grad):
    row_count, width = hidden.shape
    kv_width = value_win.shape[1]
    rank = low_out.shape[0]
    ctx_size, tp_size = lax.axis_size("ctx"), lax.axis_size("tp")
    first_share = -(-2 * width // (128 * ctx_size)) * 128
    second_share = -(-(width + kv_width) // (128 * ctx_size)) * 128
    whole = pl.BlockSpec(memory_space=pltpu.VMEM)
    f32, bf16 = jnp.float32, jnp.bfloat16

    def reduction(share):
        return [
            pltpu.VMEM((rank, share * ctx_size), bf16),
            pltpu.VMEM((ctx_size - 1, rank, share), bf16),
            pltpu.VMEM((rank, share), bf16),
            pltpu.VMEM((rank, share * ctx_size), bf16),
        ]

    return pl.pallas_call(
        finish_kernel,
        in_specs=[whole] * 8,
        out_specs=[whole] * 6,
        out_shape=[
            jax.ShapeDtypeStruct((rank, row_count), bf16),
            jax.ShapeDtypeStruct((rank, row_count), bf16),
            jax.ShapeDtypeStruct((rank, width), f32),
            jax.ShapeDtypeStruct((rank, kv_width), f32),
            jax.ShapeDtypeStruct((rank, width), f32),
            jax.ShapeDtypeStruct((rank, width), f32),
        ],
        scratch_shapes=[
            pltpu.VMEM((3, row_count, kv_width), bf16),
            pltpu.VMEM((tp_size - 1, rank, row_count), f32),
            pltpu.VMEM((rank, row_count), f32),
            pltpu.VMEM((tp_size - 1, rank, row_count), f32),
            *reduction(first_share),
            *reduction(second_share),
            dma_sems(3),
            dma_sems(3),
            *[dma_sems(tp_size - 1)] * 4,
            *[dma_sems(ctx_size - 1)] * 8,
        ],
        compiler_params=pltpu.CompilerParams(
            collective_id=1, has_side_effects=True, vmem_limit_bytes=40 * 1024 * 1024
        ),
    )(value_win, low_out, hidden, cot, value_up, low_v, weight, down_grad)


def shards(
    hidden,
    queries,
    rotated_keys,
    frozen_value_rows,
    adapter_a_v,
    value_up_matrix,
    adapter_a_o,
    output_up_matrix,
    doc_lengths,
    pair_slots,
    token_logratio,
    out_cotangent,
    attn_cotangent,
):
    row_count = hidden.shape[0]
    doc_count = doc_lengths.shape[0]
    first_row = lax.axis_index("ctx") * row_count
    doc_ends = jnp.cumsum(doc_lengths)
    query_pos = first_row + jnp.arange(row_count, dtype=jnp.int32)
    query_doc = doc_index(query_pos, doc_ends)
    reach, starts = tile_reach(first_row, row_count, doc_ends)
    key_window, value_window, low_v_t, grad_sum_t, margins = begin(
        hidden,
        adapter_a_v.T,
        out_cotangent,
        output_up_matrix,
        rotated_keys,
        frozen_value_rows,
        value_up_matrix,
        token_logratio[None, :],
        (doc_ends - doc_lengths)[:, None],
        doc_ends[:, None],
    )
    onehot = (query_doc[:, None] == jnp.arange(doc_count, dtype=jnp.int32)[None, :]).astype(
        jnp.float32
    )
    token_weight = jnp.sum(onehot * doc_weights(margins[:, 0], pair_slots)[None, :], axis=1)
    low_grad_t = (ADAPTER_SCALE * token_weight[None, :] * grad_sum_t).astype(jnp.bfloat16)
    attention_output_rows, value_terms, low_out_t, down_grad_t = attention(
        reach,
        queries,
        key_window,
        value_window,
        attn_cotangent,
        token_weight[:, None],
        low_grad_t,
        adapter_a_o.T,
        starts,
    )
    low_o_t, low_v_grad_t, value_down_t, value_up_gradient, output_down_t, output_up_gradient = (
        finish(
            value_terms,
            low_out_t,
            hidden,
            out_cotangent,
            value_up_matrix,
            low_v_t,
            token_weight[None, :],
            down_grad_t,
        )
    )
    output_adapter_term = (ADAPTER_SCALE * row_contraction(low_o_t, output_up_matrix)).astype(
        jnp.bfloat16
    )
    input_adapter_gradient = row_contraction(low_v_grad_t, adapter_a_v.T).astype(jnp.bfloat16)
    return (
        attention_output_rows,
        output_adapter_term,
        input_adapter_gradient,
        value_down_t.T,
        value_up_gradient,
        output_down_t.T,
        output_up_gradient,
    )


def solution(mesh):
    in_specs = (
        P("ctx", "tp"),
        P("ctx", "tp"),
        P("ctx", "tp"),
        P("ctx", "tp"),
        P("tp", None),
        P(None, "tp"),
        P("tp", None),
        P(None, "tp"),
        P(),
        P(),
        P("ctx"),
        P("ctx", "tp"),
        P("ctx", "tp"),
    )
    out_specs = (
        P("ctx", "tp"),
        P("ctx", "tp"),
        P("ctx", "tp"),
        P("tp", None),
        P(None, "tp"),
        P("tp", None),
        P(None, "tp"),
    )
    return jax.shard_map(shards, mesh=mesh, in_specs=in_specs, out_specs=out_specs, check_vma=False)
```

```python
import math

import jax
import jax.numpy as jnp
from jax import lax
from jax.experimental import pallas as pl
from jax.experimental.pallas import tpu as pltpu
from jax.sharding import PartitionSpec as P

HEADS = 64
KV_HEADS = 8
HD = 128


ADAPTER_SCALE = 2.0
BETA = 0.5
NEG_FILL = -1e30


def score_block(left, right):
    return lax.dot_general(
        left, right, (((1,), (1,)), ((), ())), preferred_element_type=jnp.float32
    )


def row_contraction(left, right):
    return lax.dot_general(
        left, right, (((0,), (0,)), ((), ())), preferred_element_type=jnp.float32
    )

TILE = 256
STEP_HEADS = 4
VMEM_LIMIT = 58 * 1024 * 1024
EXP2_SCALE = 1.4426950408889634 / math.sqrt(HD)


def attention_kernel(
    lengths_ref,
    query_ref,
    key_ref,
    value_ref,
    cot_ref,
    weight_ref,
    low_grad_t_ref,
    down_t_ref,
    start_ref,
    out_ref,
    value_grad_ref,
    low_out_ref,
    down_grad_ref,
    bias,
    scores,
    weights,
    grads,
    value_t,
    value_acc,
):
    step = pl.program_id(0)
    steps_per_kv = HEADS // KV_HEADS // STEP_HEADS
    row_count = query_ref.shape[0]
    window = key_ref.shape[0]
    tiles = window // TILE
    query_tiles = row_count // TILE

    first_row = lax.axis_index("ctx") * row_count

    def tile_reach(qt):
        position = first_row + qt * TILE

        def pass_doc(doc, carried):
            end = carried[0] + lengths_ref[doc]
            return end, jnp.where(end <= position, end, carried[1])

        zero = jnp.int32(0)
        start = lax.fori_loop(0, lengths_ref.shape[0], pass_doc, (zero, zero))[1]
        first = (start - first_row + window - row_count) // TILE
        return first, (window - row_count) // TILE + qt - first + 1

    @pl.when(step == 0)
    def _():
        low_out_ref[...] = jnp.zeros_like(low_out_ref)

        @pl.loop(0, query_tiles)
        def _(qt):
            first, count = tile_reach(qt)
            lane = pl.ds(pl.multiple_of(qt * TILE, TILE), TILE)
            starts = start_ref[:, lane]
            query_pos = (
                window - row_count + qt * TILE + lax.broadcasted_iota(jnp.int32, (1, TILE), 1)
            )

            @pl.loop(0, count)
            def _(k):
                key_pos = (first + k) * TILE + lax.broadcasted_iota(
                    jnp.int32, (TILE, TILE), 0
                )
                allowed = (key_pos >= starts) & (key_pos <= query_pos)
                rows = pl.ds(pl.multiple_of(k * TILE, TILE), TILE)
                bias[qt, rows, :] = jnp.where(allowed, 0.0, NEG_FILL)

    @pl.when(step % steps_per_kv == 0)
    def _():
        value_acc[...] = jnp.zeros_like(value_acc)
        for k in range(tiles):
            rows = slice(k * TILE, (k + 1) * TILE)
            value_t[:, rows] = jnp.transpose(value_ref[rows, :].astype(jnp.float32)).astype(
                jnp.bfloat16
            )

    def heads(qt, first, count):
        rows = pl.ds(pl.multiple_of(qt * TILE, TILE), TILE)
        columns = [slice(h * HD, (h + 1) * HD) for h in range(STEP_HEADS)]
        lanes = [slice(h * TILE, (h + 1) * TILE) for h in range(STEP_HEADS)]

        def key_rows(k):
            return pl.ds(pl.multiple_of((first + k) * TILE, TILE), TILE)

        tops = [jnp.full((8, TILE), NEG_FILL, jnp.float32)] * STEP_HEADS
        for k in range(count):
            span = slice(k * TILE, (k + 1) * TILE)
            for h in range(STEP_HEADS):
                block = (
                    score_block(key_ref[key_rows(k), :], query_ref[rows, columns[h]])
                    + bias[qt, span, :]
                )
                scores[span, lanes[h]] = block
                tops[h] = jnp.maximum(
                    tops[h], jnp.max(block.reshape(TILE // 8, 8, TILE), axis=0)
                )
        tops = [jnp.max(top, axis=0, keepdims=True) * EXP2_SCALE for top in tops]
        totals = [jnp.zeros((8, TILE), jnp.float32)] * STEP_HEADS
        for k in range(count):
            span = slice(k * TILE, (k + 1) * TILE)
            for h in range(STEP_HEADS):
                block = jnp.exp2(scores[span, lanes[h]] * EXP2_SCALE - tops[h])
                totals[h] = totals[h] + jnp.sum(block.reshape(TILE // 8, 8, TILE), axis=0)
                weights[span, lanes[h]] = block.astype(jnp.bfloat16)
        inverses = [1.0 / jnp.sum(total, axis=0, keepdims=True) for total in totals]
        for h in range(STEP_HEADS):
            inverse_rows = jnp.transpose(jnp.broadcast_to(inverses[h], (HD, TILE)))
            grad = weight_ref[rows, :] * cot_ref[rows, columns[h]].astype(
                jnp.float32
            ) + row_contraction(low_grad_t_ref[:, rows], down_t_ref[:, columns[h]])
            grads[lanes[h], :] = (grad * inverse_rows).astype(jnp.bfloat16)
        for h in range(STEP_HEADS):
            output = jnp.zeros((HD, TILE), jnp.float32)
            for k in range(count):
                span = slice(k * TILE, (k + 1) * TILE)
                output = output + jnp.dot(
                    value_t[:, key_rows(k)],
                    weights[span, lanes[h]],
                    preferred_element_type=jnp.float32,
                )
            out_ref[rows, columns[h]] = jnp.transpose(output * inverses[h]).astype(jnp.bfloat16)
        for k in range(count):
            span = slice(k * TILE, (k + 1) * TILE)
            value_acc[key_rows(k), :] += jnp.dot(
                weights[span, :], grads[...], preferred_element_type=jnp.float32
            )

    @pl.loop(0, query_tiles)
    def _(qt):
        first, count = tile_reach(qt)
        for variant in range(1, tiles + 1):

            @pl.when(count == variant)
            def _():
                heads(qt, first, variant)

    low_out_ref[...] += lax.dot_general(
        down_t_ref[...],
        out_ref[...],
        (((1,), (1,)), ((), ())),
        preferred_element_type=jnp.float32,
    )
    down_grad_ref[...] = jnp.dot(
        low_grad_t_ref[...], out_ref[...], preferred_element_type=jnp.float32
    )

    @pl.when(step % steps_per_kv == steps_per_kv - 1)
    def _():
        value_grad_ref[...] = value_acc[...].astype(value_grad_ref.dtype)


def attention(lengths, queries, keys, values, cot, weight, low_grad_t, down_t, starts):
    row_count, width = queries.shape
    window = keys.shape[0]
    rank = low_grad_t.shape[0]
    block = STEP_HEADS * HD
    steps = width // block
    steps_per_kv = HEADS // KV_HEADS // STEP_HEADS
    by_step = lambda i, lengths: (0, i)
    by_kv = lambda i, lengths: (0, i // steps_per_kv)
    whole = lambda i, lengths: (0, 0)
    return pl.pallas_call(
        attention_kernel,
        grid_spec=pltpu.PrefetchScalarGridSpec(
            num_scalar_prefetch=1,
            grid=(steps,),
            in_specs=[
                pl.BlockSpec((row_count, block), by_step),
                pl.BlockSpec((window, HD), by_kv),
                pl.BlockSpec((window, HD), by_kv),
                pl.BlockSpec((row_count, block), by_step),
                pl.BlockSpec((row_count, HD), whole),
                pl.BlockSpec((rank, row_count), whole),
                pl.BlockSpec((rank, block), by_step),
                pl.BlockSpec((1, row_count), whole),
            ],
            out_specs=[
                pl.BlockSpec((row_count, block), by_step),
                pl.BlockSpec((window, HD), by_kv),
                pl.BlockSpec((rank, row_count), whole),
                pl.BlockSpec((rank, block), by_step),
            ],
            scratch_shapes=[
                pltpu.VMEM((row_count // TILE, window, TILE), jnp.float32),
                pltpu.VMEM((window, STEP_HEADS * TILE), jnp.float32),
                pltpu.VMEM((window, STEP_HEADS * TILE), jnp.bfloat16),
                pltpu.VMEM((STEP_HEADS * TILE, HD), jnp.bfloat16),
                pltpu.VMEM((HD, window), jnp.bfloat16),
                pltpu.VMEM((window, HD), jnp.float32),
            ],
        ),
        out_shape=[
            jax.ShapeDtypeStruct((row_count, width), jnp.bfloat16),
            jax.ShapeDtypeStruct(keys.shape, jnp.bfloat16),
            jax.ShapeDtypeStruct((rank, row_count), jnp.float32),
            jax.ShapeDtypeStruct((rank, width), jnp.float32),
        ],
        compiler_params=pltpu.CompilerParams(vmem_limit_bytes=VMEM_LIMIT),
    )(lengths, queries, keys, values, cot, weight, low_grad_t, down_t, starts)


MESH = pl.DeviceIdType.MESH


def greet_all():
    barrier = pltpu.get_barrier_semaphore()
    count = 0
    for axis in ("ctx", "tp"):
        size = lax.axis_size(axis)
        place = lax.axis_index(axis)
        for hop in range(1, size):
            pl.semaphore_signal(
                barrier, inc=1, device_id={axis: (place + hop) % size}, device_id_type=MESH
            )
            count += 1
    pl.semaphore_wait(barrier, count)


def send_to(axis, place, source, target, send_sem, recv_sem):
    return pltpu.make_async_remote_copy(
        src_ref=source,
        dst_ref=target,
        send_sem=send_sem,
        recv_sem=recv_sem,
        device_id={axis: place},
        device_id_type=MESH,
    )


def send_round(axis, source, slots, send_sems, recv_sems):
    size = lax.axis_size(axis)
    place = lax.axis_index(axis)
    copies = []
    for hop in range(1, size):
        copy = send_to(
            axis,
            (place + hop) % size,
            source((place + hop) % size),
            slots(hop),
            send_sems.at[hop - 1],
            recv_sems.at[hop - 1],
        )
        copy.start()
        copies.append(copy)
    return copies


def slot_total(own, copies, slots):
    total = own.astype(jnp.float32)
    for hop, copy in enumerate(copies):
        copy.wait_recv()
        total = total + slots[hop].astype(jnp.float32)
    return total


def begin_kernel(
    hidden_ref,
    down_v_t_ref,
    cot_ref,
    up_ref,
    key_ref,
    frozen_ref,
    value_up_ref,
    ratio_ref,
    lengths_ref,
    slots_ref,
    key_win_ref,
    value_win_ref,
    low_v_ref,
    low_grad_ref,
    weight_ref,
    weight_rows_ref,
    start_ref,
    hidden,
    cot,
    pack,
    pack_slots,
    margin_own,
    margin_slots,
    frozen_slots,
    low_slots,
    pack_send,
    pack_recv,
    margin_send,
    margin_recv,
    rows_send,
    rows_recv,
    low_send,
    low_recv,
    load_sems,
):
    ctx_size = lax.axis_size("ctx")
    place = lax.axis_index("ctx")
    loads = [
        pltpu.make_async_copy(hidden_ref, hidden, load_sems.at[0]),
        pltpu.make_async_copy(cot_ref, cot, load_sems.at[1]),
    ]
    for load in loads:
        load.start()
    row_count = hidden_ref.shape[0]
    rank = down_v_t_ref.shape[0]
    odd = place % 2
    greet_all()

    def window_rows(slot):
        return pl.ds(pl.multiple_of(slot * row_count, row_count), row_count)

    def row_copies(sources, peer, slot, sem):
        targets = (key_win_ref.at[window_rows(slot), :], frozen_slots.at[slot])
        return [
            send_to(
                "ctx",
                jnp.minimum(peer, ctx_size - 1),
                sources[which],
                targets[which],
                rows_send.at[sem, which],
                rows_recv.at[slot, which],
            )
            for which in range(2)
        ]

    own = (key_ref, frozen_ref)
    near = row_copies(own, place + 1, 2, 0)
    far = row_copies(own, place + 2 + odd, 1 - odd, 1)
    near_on = place + 1 < ctx_size
    far_on = place + 2 + odd < ctx_size

    def passed_on(slot):
        sources = (key_win_ref.at[window_rows(slot), :], frozen_slots.at[slot])
        return row_copies(sources, place + 1, slot - 1, 1 + slot)

    def pass_on(slot):
        return (odd == 0) & near_on & (place >= 3 - slot)

    @pl.when(far_on)
    def _():
        for copy in far:
            copy.start()

    @pl.when(near_on)
    def _():
        for copy in near:
            copy.start()

    for slot in range(3):

        @pl.when(place < 3 - slot)
        def _():
            key_win_ref[slot * row_count : (slot + 1) * row_count, :] = jnp.zeros(
                key_ref.shape, key_ref.dtype
            )
            frozen_slots[slot] = jnp.zeros(frozen_ref.shape, frozen_ref.dtype)
            low_slots[slot] = jnp.zeros(low_v_ref.shape, low_v_ref.dtype)

    docs = lengths_ref.shape[1]
    by_row = lax.broadcasted_iota(jnp.int32, (docs, docs), 0)
    by_lane = lax.broadcasted_iota(jnp.int32, (docs, docs), 1)
    ends = jnp.sum(jnp.where(by_lane <= by_row, lengths_ref[...], 0), axis=1, keepdims=True)
    begins = jnp.sum(jnp.where(by_lane < by_row, lengths_ref[...], 0), axis=1, keepdims=True)
    positions = place * row_count + lax.broadcasted_iota(jnp.int32, (docs, row_count), 1)
    member = (positions >= begins) & (positions < ends)
    start_ref[...] = jnp.sum(jnp.where(member, begins, 0), axis=0, keepdims=True) - (
        place - 3
    ) * row_count
    margins = jnp.sum(jnp.where(member, ratio_ref[...], 0.0), axis=1, keepdims=True)
    margin_own[...] = jnp.broadcast_to(margins, margin_own.shape)
    margin_copies = send_round(
        "ctx", lambda peer: margin_own, lambda hop: margin_slots.at[hop - 1], margin_send, margin_recv
    )
    for load in loads:
        load.wait()
    pack[0:rank, :] = score_block(down_v_t_ref[...], hidden[...])
    pack[rank : 2 * rank, :] = score_block(up_ref[...], cot[...])
    pack_copies = send_round(
        "tp", lambda peer: pack, lambda hop: pack_slots.at[hop - 1], pack_send, pack_recv
    )
    key_win_ref[3 * row_count : 4 * row_count, :] = key_ref[...]
    sums = slot_total(pack[...], pack_copies, pack_slots)
    low_v_ref[...] = sums[0:rank, :].astype(jnp.bfloat16)
    low_copies = [
        send_to(
            "ctx",
            jnp.minimum(place + hop, ctx_size - 1),
            low_v_ref,
            low_slots.at[3 - hop],
            low_send.at[hop - 1],
            low_recv.at[hop - 1],
        )
        for hop in range(1, 4)
    ]
    for hop in range(1, 4):

        @pl.when(place + hop < ctx_size)
        def _():
            low_copies[hop - 1].start()

    for slot in (2, 1):

        @pl.when(pass_on(slot))
        def _():
            for which in range(2):
                row_copies(own, place + 1, slot, 0)[which].wait_recv()
            for copy in passed_on(slot):
                copy.start()

    margins = slot_total(margin_own[...], margin_copies, margin_slots)[:, 0:1]
    slot_column = jnp.sum(jnp.where(by_row == by_lane, slots_ref[...], 0), axis=1, keepdims=True)
    sign_column = jnp.where(slot_column % 2 == 0, 1.0, -1.0)
    signed_row = jnp.sum(
        jnp.where(by_row == by_lane, sign_column * margins, 0.0), axis=0, keepdims=True
    )
    gaps = jnp.sum(
        jnp.where(slot_column // 2 == slots_ref[...] // 2, signed_row, 0.0), axis=1, keepdims=True
    )
    doc_weight = -BETA * sign_column * jax.nn.sigmoid(-BETA * gaps)
    weight = jnp.sum(jnp.where(member, doc_weight, 0.0), axis=0, keepdims=True)
    weight_ref[...] = weight
    weight_rows_ref[...] = jnp.transpose(jnp.broadcast_to(weight, (HD, row_count)))
    low_grad_ref[...] = (ADAPTER_SCALE * weight * sums[rank : 2 * rank, :]).astype(jnp.bfloat16)

    def rows_of(low, frozen):
        return (
            frozen.astype(jnp.float32) + ADAPTER_SCALE * row_contraction(low, value_up_ref[...])
        ).astype(jnp.bfloat16)

    value_win_ref[3 * row_count : 4 * row_count, :] = rows_of(low_v_ref[...], frozen_ref[...])
    for slot in (2, 1, 0):

        @pl.when(place >= 3 - slot)
        def _():
            low_copies[2 - slot].wait_recv()

        already = pass_on(slot) if slot > 0 else place < 0

        @pl.when((place >= 3 - slot) & jnp.logical_not(already))
        def _():
            for which in range(2):
                row_copies(own, place + 1, slot, 0)[which].wait_recv()

        value_win_ref[slot * row_count : (slot + 1) * row_count, :] = rows_of(
            low_slots[slot], frozen_slots[slot]
        )

    @pl.when(far_on)
    def _():
        for copy in far:
            copy.wait_send()

    @pl.when(near_on)
    def _():
        for copy in near:
            copy.wait_send()

    for slot in (2, 1):

        @pl.when(pass_on(slot))
        def _():
            for copy in passed_on(slot):
                copy.wait_send()

    for hop in range(1, 4):

        @pl.when(place + hop < ctx_size)
        def _():
            low_copies[hop - 1].wait_send()

    for copy in margin_copies + pack_copies:
        copy.wait_send()


def dma_sems(*shape):
    return pltpu.SemaphoreType.DMA(shape)


def begin(hidden, down_v_t, cot, up, keys, frozen, value_up, ratio, lengths, slots):
    row_count = hidden.shape[0]
    rank = up.shape[0]
    docs = lengths.shape[1]
    ctx_size, tp_size = lax.axis_size("ctx"), lax.axis_size("tp")
    window = (4 * row_count, keys.shape[1])
    whole = pl.BlockSpec(memory_space=pltpu.VMEM)
    far = pl.BlockSpec(memory_space=pl.ANY)
    f32, bf16 = jnp.float32, jnp.bfloat16
    return pl.pallas_call(
        begin_kernel,
        in_specs=[far, whole, far] + [whole] * 7,
        out_specs=[whole] * 7,
        out_shape=[
            jax.ShapeDtypeStruct(window, bf16),
            jax.ShapeDtypeStruct(window, bf16),
            jax.ShapeDtypeStruct((rank, row_count), bf16),
            jax.ShapeDtypeStruct((rank, row_count), bf16),
            jax.ShapeDtypeStruct((1, row_count), f32),
            jax.ShapeDtypeStruct((row_count, HD), f32),
            jax.ShapeDtypeStruct((1, row_count), jnp.int32),
        ],
        scratch_shapes=[
            pltpu.VMEM(hidden.shape, bf16),
            pltpu.VMEM(cot.shape, bf16),
            pltpu.VMEM((2 * rank, row_count), f32),
            pltpu.VMEM((tp_size - 1, 2 * rank, row_count), f32),
            pltpu.VMEM((docs, 128), f32),
            pltpu.VMEM((ctx_size - 1, docs, 128), f32),
            pltpu.VMEM((3, row_count, keys.shape[1]), bf16),
            pltpu.VMEM((3, rank, row_count), bf16),
            dma_sems(tp_size - 1),
            dma_sems(tp_size - 1),
            dma_sems(ctx_size - 1),
            dma_sems(ctx_size - 1),
            dma_sems(4, 2),
            dma_sems(3, 2),
            dma_sems(3),
            dma_sems(3),
            dma_sems(2),
        ],
        compiler_params=pltpu.CompilerParams(
            collective_id=0, has_side_effects=True, vmem_limit_bytes=VMEM_LIMIT
        ),
    )(hidden, down_v_t, cot, up, keys, frozen, value_up, ratio, lengths, slots)


def finish_kernel(
    value_win_ref,
    low_out_ref,
    hidden_ref,
    cot_ref,
    value_up_ref,
    low_v_ref,
    weight_ref,
    down_grad_ref,
    low_o_ref,
    low_v_grad_ref,
    value_down_ref,
    value_up_grad_ref,
    output_down_ref,
    output_up_ref,
    value_slots,
    low_out_slots,
    low_grad_own,
    low_grad_slots,
    first_own,
    first_slots,
    first_part,
    first_sum,
    second_own,
    second_slots,
    second_part,
    second_sum,
    value_send,
    value_recv,
    low_out_send,
    low_out_recv,
    low_grad_send,
    low_grad_recv,
    first_send,
    first_recv,
    first_back_send,
    first_back_recv,
    second_send,
    second_recv,
    second_back_send,
    second_back_recv,
):
    ctx_size = lax.axis_size("ctx")
    place = lax.axis_index("ctx")
    row_count, width = hidden_ref.shape
    kv_width = value_win_ref.shape[1]
    greet_all()
    low_out_copies = send_round(
        "tp",
        lambda peer: low_out_ref,
        lambda hop: low_out_slots.at[hop - 1],
        low_out_send,
        low_out_recv,
    )
    value_copies = [
        send_to(
            "ctx",
            jnp.maximum(place - hop, 0),
            value_win_ref.at[(3 - hop) * row_count : (4 - hop) * row_count, :],
            value_slots.at[hop - 1],
            value_send.at[hop - 1],
            value_recv.at[hop - 1],
        )
        for hop in range(1, 4)
    ]
    for hop in (3, 2, 1):

        @pl.when(place >= hop)
        def _():
            value_copies[hop - 1].start()

    for hop in range(1, 4):

        @pl.when(place + hop >= ctx_size)
        def _():
            value_slots[hop - 1] = jnp.zeros(value_slots.shape[1:], value_slots.dtype)

    def columns(own, part):
        share = own.shape[1] // ctx_size
        return pl.ds(pl.multiple_of(part * share, 128), share)

    def scatter(own, slots, sends, recvs):
        return send_round(
            "ctx",
            lambda peer: own.at[:, columns(own, peer)],
            lambda hop: slots.at[hop - 1],
            sends,
            recvs,
        )

    def gather(own, copies, slots, part, total, sends, recvs):
        mine = columns(own, place)
        part[...] = slot_total(own[:, mine], copies, slots).astype(jnp.bfloat16)
        total[:, mine] = part[...]
        return send_round(
            "ctx", lambda peer: part, lambda hop: total.at[:, mine], sends, recvs
        )

    def gathered(copies, total, recvs):
        for hop, copy in enumerate(copies):
            peer = (place + ctx_size - hop - 1) % ctx_size
            send_to(
                "ctx", (place + 1) % ctx_size, total.at[:, columns(total, peer)],
                total.at[:, columns(total, peer)], recvs.at[hop], recvs.at[hop],
            ).wait_recv()

    if first_own.shape[1] > 2 * width:
        first_own[:, 2 * width :] = jnp.zeros(
            (first_own.shape[0], first_own.shape[1] - 2 * width), jnp.bfloat16
        )
    if second_own.shape[1] > width + kv_width:
        second_own[:, width + kv_width :] = jnp.zeros(
            (second_own.shape[0], second_own.shape[1] - width - kv_width), jnp.bfloat16
        )
    first_own[:, 0:width] = down_grad_ref[...].astype(jnp.bfloat16)
    low_o = slot_total(low_out_ref[...], low_out_copies, low_out_slots).astype(jnp.bfloat16)
    low_o_ref[...] = low_o
    weighted = (ADAPTER_SCALE * weight_ref[...] * low_o.astype(jnp.float32)).astype(jnp.bfloat16)
    first_own[:, width : 2 * width] = jnp.dot(
        weighted, cot_ref[...], preferred_element_type=jnp.float32
    ).astype(jnp.bfloat16)
    first_copies = scatter(first_own, first_slots, first_send, first_recv)
    total = value_win_ref[3 * row_count : 4 * row_count, :].astype(jnp.float32)
    for hop in range(1, 4):

        @pl.when(place + hop < ctx_size)
        def _():
            value_copies[hop - 1].wait_recv()

        total = total + value_slots[hop - 1].astype(jnp.float32)
    value_grad = total.astype(jnp.bfloat16)
    low_grad_own[...] = ADAPTER_SCALE * score_block(value_up_ref[...], value_grad)
    low_grad_copies = send_round(
        "tp",
        lambda peer: low_grad_own,
        lambda hop: low_grad_slots.at[hop - 1],
        low_grad_send,
        low_grad_recv,
    )
    second_own[:, width : width + kv_width] = (
        ADAPTER_SCALE * jnp.dot(low_v_ref[...], value_grad, preferred_element_type=jnp.float32)
    ).astype(jnp.bfloat16)
    first_back = gather(
        first_own, first_copies, first_slots, first_part, first_sum, first_back_send, first_back_recv
    )
    low_grad = slot_total(low_grad_own[...], low_grad_copies, low_grad_slots).astype(jnp.bfloat16)
    low_v_grad_ref[...] = low_grad
    second_own[:, 0:width] = jnp.dot(
        low_grad, hidden_ref[...], preferred_element_type=jnp.float32
    ).astype(jnp.bfloat16)
    second_copies = scatter(second_own, second_slots, second_send, second_recv)
    gathered(first_back, first_sum, first_back_recv)
    output_down_ref[...] = first_sum[:, 0:width].astype(jnp.float32)
    output_up_ref[...] = first_sum[:, width : 2 * width].astype(jnp.float32)
    second_back = gather(
        second_own,
        second_copies,
        second_slots,
        second_part,
        second_sum,
        second_back_send,
        second_back_recv,
    )
    gathered(second_back, second_sum, second_back_recv)
    value_down_ref[...] = second_sum[:, 0:width].astype(jnp.float32)
    value_up_grad_ref[...] = second_sum[:, width : width + kv_width].astype(jnp.float32)
    for hop in range(1, 4):

        @pl.when(place >= hop)
        def _():
            value_copies[hop - 1].wait_send()

    for copies in (
        low_out_copies,
        low_grad_copies,
        first_copies,
        first_back,
        second_copies,
        second_back,
    ):
        for copy in copies:
            copy.wait_send()


def finish(value_win, low_out, hidden, cot, value_up, low_v, weight, down_grad):
    row_count, width = hidden.shape
    kv_width = value_win.shape[1]
    rank = low_out.shape[0]
    ctx_size, tp_size = lax.axis_size("ctx"), lax.axis_size("tp")
    first_share = -(-2 * width // (128 * ctx_size)) * 128
    second_share = -(-(width + kv_width) // (128 * ctx_size)) * 128
    whole = pl.BlockSpec(memory_space=pltpu.VMEM)
    f32, bf16 = jnp.float32, jnp.bfloat16

    def reduction(share):
        return [
            pltpu.VMEM((rank, share * ctx_size), bf16),
            pltpu.VMEM((ctx_size - 1, rank, share), bf16),
            pltpu.VMEM((rank, share), bf16),
            pltpu.VMEM((rank, share * ctx_size), bf16),
        ]

    return pl.pallas_call(
        finish_kernel,
        in_specs=[whole] * 8,
        out_specs=[whole] * 6,
        out_shape=[
            jax.ShapeDtypeStruct((rank, row_count), bf16),
            jax.ShapeDtypeStruct((rank, row_count), bf16),
            jax.ShapeDtypeStruct((rank, width), f32),
            jax.ShapeDtypeStruct((rank, kv_width), f32),
            jax.ShapeDtypeStruct((rank, width), f32),
            jax.ShapeDtypeStruct((rank, width), f32),
        ],
        scratch_shapes=[
            pltpu.VMEM((3, row_count, kv_width), bf16),
            pltpu.VMEM((tp_size - 1, rank, row_count), f32),
            pltpu.VMEM((rank, row_count), f32),
            pltpu.VMEM((tp_size - 1, rank, row_count), f32),
            *reduction(first_share),
            *reduction(second_share),
            dma_sems(3),
            dma_sems(3),
            *[dma_sems(tp_size - 1)] * 4,
            *[dma_sems(ctx_size - 1)] * 8,
        ],
        compiler_params=pltpu.CompilerParams(
            collective_id=1, has_side_effects=True, vmem_limit_bytes=VMEM_LIMIT
        ),
    )(value_win, low_out, hidden, cot, value_up, low_v, weight, down_grad)


def shards(
    hidden,
    queries,
    rotated_keys,
    frozen_value_rows,
    adapter_a_v,
    value_up_matrix,
    adapter_a_o,
    output_up_matrix,
    doc_lengths,
    pair_slots,
    token_logratio,
    out_cotangent,
    attn_cotangent,
):
    key_window, value_window, low_v_t, low_grad_t, weight, weight_rows, starts = begin(
        hidden,
        adapter_a_v.T,
        out_cotangent,
        output_up_matrix,
        rotated_keys,
        frozen_value_rows,
        value_up_matrix,
        token_logratio[None, :],
        doc_lengths[None, :],
        pair_slots[None, :],
    )
    attention_output_rows, value_terms, low_out_t, down_grad_t = attention(
        doc_lengths,
        queries,
        key_window,
        value_window,
        attn_cotangent,
        weight_rows,
        low_grad_t,
        adapter_a_o.T,
        starts,
    )
    low_o_t, low_v_grad_t, value_down_t, value_up_gradient, output_down_t, output_up_gradient = (
        finish(
            value_terms,
            low_out_t,
            hidden,
            out_cotangent,
            value_up_matrix,
            low_v_t,
            weight,
            down_grad_t,
        )
    )
    output_adapter_term = (ADAPTER_SCALE * row_contraction(low_o_t, output_up_matrix)).astype(
        jnp.bfloat16
    )
    input_adapter_gradient = row_contraction(low_v_grad_t, adapter_a_v.T).astype(jnp.bfloat16)
    return (
        attention_output_rows,
        output_adapter_term,
        input_adapter_gradient,
        value_down_t.T,
        value_up_gradient,
        output_down_t.T,
        output_up_gradient,
    )


def solution(mesh):
    in_specs = (
        P("ctx", "tp"),
        P("ctx", "tp"),
        P("ctx", "tp"),
        P("ctx", "tp"),
        P("tp", None),
        P(None, "tp"),
        P("tp", None),
        P(None, "tp"),
        P(),
        P(),
        P("ctx"),
        P("ctx", "tp"),
        P("ctx", "tp"),
    )
    out_specs = (
        P("ctx", "tp"),
        P("ctx", "tp"),
        P("ctx", "tp"),
        P("tp", None),
        P(None, "tp"),
        P("tp", None),
        P(None, "tp"),
    )
    return jax.shard_map(shards, mesh=mesh, in_specs=in_specs, out_specs=out_specs, check_vma=False)
```

```python
import math

import jax
import jax.numpy as jnp
from jax import lax
from jax.experimental import pallas as pl
from jax.experimental.pallas import tpu as pltpu
from jax.sharding import PartitionSpec as P

HEADS = 64
KV_HEADS = 8
HD = 128


ADAPTER_SCALE = 2.0
BETA = 0.5
NEG_FILL = -1e30


def score_block(left, right):
    return lax.dot_general(
        left, right, (((1,), (1,)), ((), ())), preferred_element_type=jnp.float32
    )


def row_contraction(left, right):
    return lax.dot_general(
        left, right, (((0,), (0,)), ((), ())), preferred_element_type=jnp.float32
    )

TILE = 256
STEP_HEADS = 4
VMEM_LIMIT = 58 * 1024 * 1024
EXP2_SCALE = 1.4426950408889634 / math.sqrt(HD)


def attention_kernel(
    lengths_ref,
    query_ref,
    key_ref,
    value_ref,
    cot_ref,
    weight_ref,
    low_grad_t_ref,
    down_t_ref,
    start_ref,
    out_ref,
    value_grad_ref,
    low_out_ref,
    down_grad_ref,
    bias,
    scores,
    weights,
    grads,
    value_t,
    value_acc,
):
    step = pl.program_id(0)
    steps_per_kv = HEADS // KV_HEADS // STEP_HEADS
    row_count = query_ref.shape[0]
    window = key_ref.shape[0]
    tiles = window // TILE
    query_tiles = row_count // TILE

    first_row = lax.axis_index("ctx") * row_count

    def tile_reach(qt):
        position = first_row + qt * TILE

        def pass_doc(doc, carried):
            end = carried[0] + lengths_ref[doc]
            return end, jnp.where(end <= position, end, carried[1])

        zero = jnp.int32(0)
        start = lax.fori_loop(0, lengths_ref.shape[0], pass_doc, (zero, zero))[1]
        first = (start - first_row + window - row_count) // TILE
        return first, (window - row_count) // TILE + qt - first + 1

    @pl.when(step == 0)
    def _():
        low_out_ref[...] = jnp.zeros_like(low_out_ref)

        @pl.loop(0, query_tiles)
        def _(qt):
            first, count = tile_reach(qt)
            lane = pl.ds(pl.multiple_of(qt * TILE, TILE), TILE)
            starts = start_ref[:, lane]
            query_pos = (
                window - row_count + qt * TILE + lax.broadcasted_iota(jnp.int32, (1, TILE), 1)
            )

            @pl.loop(0, count)
            def _(k):
                key_pos = (first + k) * TILE + lax.broadcasted_iota(
                    jnp.int32, (TILE, TILE), 0
                )
                allowed = (key_pos >= starts) & (key_pos <= query_pos)
                rows = pl.ds(pl.multiple_of(k * TILE, TILE), TILE)
                bias[qt, rows, :] = jnp.where(allowed, 0.0, NEG_FILL)

    @pl.when(step % steps_per_kv == 0)
    def _():
        value_acc[...] = jnp.zeros_like(value_acc)
        for k in range(tiles):
            rows = slice(k * TILE, (k + 1) * TILE)
            value_t[:, rows] = jnp.transpose(value_ref[rows, :].astype(jnp.float32)).astype(
                jnp.bfloat16
            )

    def heads(qt, first, count):
        rows = pl.ds(pl.multiple_of(qt * TILE, TILE), TILE)
        columns = [slice(h * HD, (h + 1) * HD) for h in range(STEP_HEADS)]
        lanes = [slice(h * TILE, (h + 1) * TILE) for h in range(STEP_HEADS)]

        def key_rows(k):
            return pl.ds(pl.multiple_of((first + k) * TILE, TILE), TILE)

        tops = [jnp.full((8, TILE), NEG_FILL, jnp.float32)] * STEP_HEADS
        for k in range(count):
            span = slice(k * TILE, (k + 1) * TILE)
            for h in range(STEP_HEADS):
                block = (
                    score_block(key_ref[key_rows(k), :], query_ref[rows, columns[h]])
                    + bias[qt, span, :]
                )
                scores[span, lanes[h]] = block
                tops[h] = jnp.maximum(
                    tops[h], jnp.max(block.reshape(TILE // 8, 8, TILE), axis=0)
                )
        tops = [jnp.max(top, axis=0, keepdims=True) * EXP2_SCALE for top in tops]
        totals = [jnp.zeros((8, TILE), jnp.float32)] * STEP_HEADS
        for k in range(count):
            span = slice(k * TILE, (k + 1) * TILE)
            for h in range(STEP_HEADS):
                block = jnp.exp2(scores[span, lanes[h]] * EXP2_SCALE - tops[h])
                totals[h] = totals[h] + jnp.sum(block.reshape(TILE // 8, 8, TILE), axis=0)
                weights[span, lanes[h]] = block.astype(jnp.bfloat16)
        inverses = [1.0 / jnp.sum(total, axis=0, keepdims=True) for total in totals]
        for h in range(STEP_HEADS):
            inverse_rows = jnp.transpose(jnp.broadcast_to(inverses[h], (HD, TILE)))
            grad = weight_ref[rows, :] * cot_ref[rows, columns[h]].astype(
                jnp.float32
            ) + row_contraction(low_grad_t_ref[:, rows], down_t_ref[:, columns[h]])
            grads[lanes[h], :] = (grad * inverse_rows).astype(jnp.bfloat16)
        for h in range(STEP_HEADS):
            output = jnp.zeros((HD, TILE), jnp.float32)
            for k in range(count):
                span = slice(k * TILE, (k + 1) * TILE)
                output = output + jnp.dot(
                    value_t[:, key_rows(k)],
                    weights[span, lanes[h]],
                    preferred_element_type=jnp.float32,
                )
            out_ref[rows, columns[h]] = jnp.transpose(output * inverses[h]).astype(jnp.bfloat16)
        for k in range(count):
            span = slice(k * TILE, (k + 1) * TILE)
            value_acc[key_rows(k), :] += jnp.dot(
                weights[span, :], grads[...], preferred_element_type=jnp.float32
            )

    @pl.loop(0, query_tiles)
    def _(qt):
        first, count = tile_reach(qt)
        for variant in range(1, (window - row_count) // TILE + 2):

            @pl.when(count == variant)
            def _():
                heads(qt, first, variant)

    low_out_ref[...] += lax.dot_general(
        down_t_ref[...],
        out_ref[...],
        (((1,), (1,)), ((), ())),
        preferred_element_type=jnp.float32,
    )
    down_grad_ref[...] = jnp.dot(
        low_grad_t_ref[...], out_ref[...], preferred_element_type=jnp.float32
    )

    @pl.when(step % steps_per_kv == steps_per_kv - 1)
    def _():
        value_grad_ref[...] = value_acc[...].astype(value_grad_ref.dtype)


def attention(lengths, queries, keys, values, cot, weight, low_grad_t, down_t, starts):
    row_count, width = queries.shape
    window = keys.shape[0]
    rank = low_grad_t.shape[0]
    block = STEP_HEADS * HD
    steps = width // block
    steps_per_kv = HEADS // KV_HEADS // STEP_HEADS
    by_step = lambda i, lengths: (0, i)
    by_kv = lambda i, lengths: (0, i // steps_per_kv)
    whole = lambda i, lengths: (0, 0)
    return pl.pallas_call(
        attention_kernel,
        grid_spec=pltpu.PrefetchScalarGridSpec(
            num_scalar_prefetch=1,
            grid=(steps,),
            in_specs=[
                pl.BlockSpec((row_count, block), by_step),
                pl.BlockSpec((window, HD), by_kv),
                pl.BlockSpec((window, HD), by_kv),
                pl.BlockSpec((row_count, block), by_step),
                pl.BlockSpec((row_count, HD), whole),
                pl.BlockSpec((rank, row_count), whole),
                pl.BlockSpec((rank, block), by_step),
                pl.BlockSpec((1, row_count), whole),
            ],
            out_specs=[
                pl.BlockSpec((row_count, block), by_step),
                pl.BlockSpec((window, HD), by_kv),
                pl.BlockSpec((rank, row_count), whole),
                pl.BlockSpec((rank, block), by_step),
            ],
            scratch_shapes=[
                pltpu.VMEM((row_count // TILE, window, TILE), jnp.float32),
                pltpu.VMEM((window, STEP_HEADS * TILE), jnp.float32),
                pltpu.VMEM((window, STEP_HEADS * TILE), jnp.bfloat16),
                pltpu.VMEM((STEP_HEADS * TILE, HD), jnp.bfloat16),
                pltpu.VMEM((HD, window), jnp.bfloat16),
                pltpu.VMEM((window, HD), jnp.float32),
            ],
        ),
        out_shape=[
            jax.ShapeDtypeStruct((row_count, width), jnp.bfloat16),
            jax.ShapeDtypeStruct(keys.shape, jnp.bfloat16),
            jax.ShapeDtypeStruct((rank, row_count), jnp.float32),
            jax.ShapeDtypeStruct((rank, width), jnp.float32),
        ],
        compiler_params=pltpu.CompilerParams(vmem_limit_bytes=VMEM_LIMIT),
    )(lengths, queries, keys, values, cot, weight, low_grad_t, down_t, starts)


MESH = pl.DeviceIdType.MESH


def greet_all():
    barrier = pltpu.get_barrier_semaphore()
    count = 0
    for axis in ("ctx", "tp"):
        size = lax.axis_size(axis)
        place = lax.axis_index(axis)
        for hop in range(1, size):
            pl.semaphore_signal(
                barrier, inc=1, device_id={axis: (place + hop) % size}, device_id_type=MESH
            )
            count += 1
    pl.semaphore_wait(barrier, count)


def send_to(axis, place, source, target, send_sem, recv_sem):
    return pltpu.make_async_remote_copy(
        src_ref=source,
        dst_ref=target,
        send_sem=send_sem,
        recv_sem=recv_sem,
        device_id={axis: place},
        device_id_type=MESH,
    )


def send_round(axis, source, slots, send_sems, recv_sems):
    size = lax.axis_size(axis)
    place = lax.axis_index(axis)
    copies = []
    for hop in range(1, size):
        copy = send_to(
            axis,
            (place + hop) % size,
            source((place + hop) % size),
            slots(hop),
            send_sems.at[hop - 1],
            recv_sems.at[hop - 1],
        )
        copy.start()
        copies.append(copy)
    return copies


def slot_total(own, copies, slots):
    total = own.astype(jnp.float32)
    for hop, copy in enumerate(copies):
        copy.wait_recv()
        total = total + slots[hop].astype(jnp.float32)
    return total


def begin_kernel(
    hidden_ref,
    down_v_t_ref,
    cot_ref,
    up_ref,
    key_ref,
    frozen_ref,
    value_up_ref,
    ratio_ref,
    lengths_ref,
    slots_ref,
    key_win_ref,
    value_win_ref,
    low_v_ref,
    low_grad_ref,
    weight_ref,
    weight_rows_ref,
    start_ref,
    hidden,
    cot,
    pack,
    pack_slots,
    margin_own,
    margin_slots,
    frozen_slots,
    low_slots,
    pack_send,
    pack_recv,
    margin_send,
    margin_recv,
    rows_send,
    rows_recv,
    low_send,
    low_recv,
    load_sems,
):
    ctx_size = lax.axis_size("ctx")
    place = lax.axis_index("ctx")
    loads = [
        pltpu.make_async_copy(hidden_ref, hidden, load_sems.at[0]),
        pltpu.make_async_copy(cot_ref, cot, load_sems.at[1]),
    ]
    for load in loads:
        load.start()
    row_count = hidden_ref.shape[0]
    rank = down_v_t_ref.shape[0]
    odd = place % 2
    greet_all()

    def window_rows(slot):
        return pl.ds(pl.multiple_of(slot * row_count, row_count), row_count)

    def row_copies(sources, peer, slot, sem):
        targets = (key_win_ref.at[window_rows(slot), :], frozen_slots.at[slot])
        return [
            send_to(
                "ctx",
                jnp.minimum(peer, ctx_size - 1),
                sources[which],
                targets[which],
                rows_send.at[sem, which],
                rows_recv.at[slot, which],
            )
            for which in range(2)
        ]

    own = (key_ref, frozen_ref)
    near = row_copies(own, place + 1, 2, 0)
    far = row_copies(own, place + 2 + odd, 1 - odd, 1)
    near_on = place + 1 < ctx_size
    far_on = place + 2 + odd < ctx_size

    def passed_on(slot):
        sources = (key_win_ref.at[window_rows(slot), :], frozen_slots.at[slot])
        return row_copies(sources, place + 1, slot - 1, 1 + slot)

    def pass_on(slot):
        return (odd == 0) & near_on & (place >= 3 - slot)

    @pl.when(far_on)
    def _():
        for copy in far:
            copy.start()

    @pl.when(near_on)
    def _():
        for copy in near:
            copy.start()

    for slot in range(3):

        @pl.when(place < 3 - slot)
        def _():
            key_win_ref[slot * row_count : (slot + 1) * row_count, :] = jnp.zeros(
                key_ref.shape, key_ref.dtype
            )
            frozen_slots[slot] = jnp.zeros(frozen_ref.shape, frozen_ref.dtype)
            low_slots[slot] = jnp.zeros(low_v_ref.shape, low_v_ref.dtype)

    docs = lengths_ref.shape[1]
    by_row = lax.broadcasted_iota(jnp.int32, (docs, docs), 0)
    by_lane = lax.broadcasted_iota(jnp.int32, (docs, docs), 1)
    ends = jnp.sum(jnp.where(by_lane <= by_row, lengths_ref[...], 0), axis=1, keepdims=True)
    begins = jnp.sum(jnp.where(by_lane < by_row, lengths_ref[...], 0), axis=1, keepdims=True)
    positions = place * row_count + lax.broadcasted_iota(jnp.int32, (docs, row_count), 1)
    member = (positions >= begins) & (positions < ends)
    start_ref[...] = jnp.sum(jnp.where(member, begins, 0), axis=0, keepdims=True) - (
        place - 3
    ) * row_count
    margins = jnp.sum(jnp.where(member, ratio_ref[...], 0.0), axis=1, keepdims=True)
    margin_own[...] = jnp.broadcast_to(margins, margin_own.shape)
    margin_copies = send_round(
        "ctx", lambda peer: margin_own, lambda hop: margin_slots.at[hop - 1], margin_send, margin_recv
    )
    for load in loads:
        load.wait()
    pack[0:rank, :] = score_block(down_v_t_ref[...], hidden[...])
    pack[rank : 2 * rank, :] = score_block(up_ref[...], cot[...])
    pack_copies = send_round(
        "tp", lambda peer: pack, lambda hop: pack_slots.at[hop - 1], pack_send, pack_recv
    )
    key_win_ref[3 * row_count : 4 * row_count, :] = key_ref[...]
    sums = slot_total(pack[...], pack_copies, pack_slots)
    low_v_ref[...] = sums[0:rank, :].astype(jnp.bfloat16)
    low_copies = [
        send_to(
            "ctx",
            jnp.minimum(place + hop, ctx_size - 1),
            low_v_ref,
            low_slots.at[3 - hop],
            low_send.at[hop - 1],
            low_recv.at[hop - 1],
        )
        for hop in range(1, 4)
    ]
    for hop in range(1, 4):

        @pl.when(place + hop < ctx_size)
        def _():
            low_copies[hop - 1].start()

    for slot in (2, 1):

        @pl.when(pass_on(slot))
        def _():
            for which in range(2):
                row_copies(own, place + 1, slot, 0)[which].wait_recv()
            for copy in passed_on(slot):
                copy.start()

    margins = slot_total(margin_own[...], margin_copies, margin_slots)[:, 0:1]
    slot_column = jnp.sum(jnp.where(by_row == by_lane, slots_ref[...], 0), axis=1, keepdims=True)
    sign_column = jnp.where(slot_column % 2 == 0, 1.0, -1.0)
    signed_row = jnp.sum(
        jnp.where(by_row == by_lane, sign_column * margins, 0.0), axis=0, keepdims=True
    )
    gaps = jnp.sum(
        jnp.where(slot_column // 2 == slots_ref[...] // 2, signed_row, 0.0), axis=1, keepdims=True
    )
    doc_weight = -BETA * sign_column * jax.nn.sigmoid(-BETA * gaps)
    weight = jnp.sum(jnp.where(member, doc_weight, 0.0), axis=0, keepdims=True)
    weight_ref[...] = weight
    weight_rows_ref[...] = jnp.transpose(jnp.broadcast_to(weight, (HD, row_count)))
    low_grad_ref[...] = (ADAPTER_SCALE * weight * sums[rank : 2 * rank, :]).astype(jnp.bfloat16)

    def rows_of(low, frozen):
        return (
            frozen.astype(jnp.float32) + ADAPTER_SCALE * row_contraction(low, value_up_ref[...])
        ).astype(jnp.bfloat16)

    value_win_ref[3 * row_count : 4 * row_count, :] = rows_of(low_v_ref[...], frozen_ref[...])
    for slot in (2, 1, 0):

        @pl.when(place >= 3 - slot)
        def _():
            low_copies[2 - slot].wait_recv()

        already = pass_on(slot) if slot > 0 else place < 0

        @pl.when((place >= 3 - slot) & jnp.logical_not(already))
        def _():
            for which in range(2):
                row_copies(own, place + 1, slot, 0)[which].wait_recv()

        value_win_ref[slot * row_count : (slot + 1) * row_count, :] = rows_of(
            low_slots[slot], frozen_slots[slot]
        )

    @pl.when(far_on)
    def _():
        for copy in far:
            copy.wait_send()

    @pl.when(near_on)
    def _():
        for copy in near:
            copy.wait_send()

    for slot in (2, 1):

        @pl.when(pass_on(slot))
        def _():
            for copy in passed_on(slot):
                copy.wait_send()

    for hop in range(1, 4):

        @pl.when(place + hop < ctx_size)
        def _():
            low_copies[hop - 1].wait_send()

    for copy in margin_copies + pack_copies:
        copy.wait_send()


def dma_sems(*shape):
    return pltpu.SemaphoreType.DMA(shape)


def begin(hidden, down_v_t, cot, up, keys, frozen, value_up, ratio, lengths, slots):
    row_count = hidden.shape[0]
    rank = up.shape[0]
    docs = lengths.shape[1]
    ctx_size, tp_size = lax.axis_size("ctx"), lax.axis_size("tp")
    window = (4 * row_count, keys.shape[1])
    whole = pl.BlockSpec(memory_space=pltpu.VMEM)
    far = pl.BlockSpec(memory_space=pl.ANY)
    f32, bf16 = jnp.float32, jnp.bfloat16
    return pl.pallas_call(
        begin_kernel,
        in_specs=[far, whole, far] + [whole] * 7,
        out_specs=[whole] * 7,
        out_shape=[
            jax.ShapeDtypeStruct(window, bf16),
            jax.ShapeDtypeStruct(window, bf16),
            jax.ShapeDtypeStruct((rank, row_count), bf16),
            jax.ShapeDtypeStruct((rank, row_count), bf16),
            jax.ShapeDtypeStruct((1, row_count), f32),
            jax.ShapeDtypeStruct((row_count, HD), f32),
            jax.ShapeDtypeStruct((1, row_count), jnp.int32),
        ],
        scratch_shapes=[
            pltpu.VMEM(hidden.shape, bf16),
            pltpu.VMEM(cot.shape, bf16),
            pltpu.VMEM((2 * rank, row_count), f32),
            pltpu.VMEM((tp_size - 1, 2 * rank, row_count), f32),
            pltpu.VMEM((docs, 128), f32),
            pltpu.VMEM((ctx_size - 1, docs, 128), f32),
            pltpu.VMEM((3, row_count, keys.shape[1]), bf16),
            pltpu.VMEM((3, rank, row_count), bf16),
            dma_sems(tp_size - 1),
            dma_sems(tp_size - 1),
            dma_sems(ctx_size - 1),
            dma_sems(ctx_size - 1),
            dma_sems(4, 2),
            dma_sems(3, 2),
            dma_sems(3),
            dma_sems(3),
            dma_sems(2),
        ],
        compiler_params=pltpu.CompilerParams(
            collective_id=0, has_side_effects=True, vmem_limit_bytes=VMEM_LIMIT
        ),
    )(hidden, down_v_t, cot, up, keys, frozen, value_up, ratio, lengths, slots)


def finish_kernel(
    value_win_ref,
    low_out_ref,
    hidden_ref,
    cot_ref,
    value_up_ref,
    low_v_ref,
    weight_ref,
    down_grad_ref,
    low_o_ref,
    low_v_grad_ref,
    value_down_ref,
    value_up_grad_ref,
    output_down_ref,
    output_up_ref,
    hidden,
    cot,
    value_slots,
    low_out_slots,
    low_grad_own,
    low_grad_slots,
    first_own,
    first_slots,
    first_part,
    first_sum,
    second_own,
    second_slots,
    second_part,
    second_sum,
    value_send,
    value_recv,
    low_out_send,
    low_out_recv,
    low_grad_send,
    low_grad_recv,
    first_send,
    first_recv,
    first_back_send,
    first_back_recv,
    second_send,
    second_recv,
    second_back_send,
    second_back_recv,
    load_sems,
):
    ctx_size = lax.axis_size("ctx")
    place = lax.axis_index("ctx")
    loads = [
        pltpu.make_async_copy(cot_ref, cot, load_sems.at[0]),
        pltpu.make_async_copy(hidden_ref, hidden, load_sems.at[1]),
    ]
    for load in loads:
        load.start()
    row_count, width = hidden_ref.shape
    kv_width = value_win_ref.shape[1]
    greet_all()
    low_out_copies = send_round(
        "tp",
        lambda peer: low_out_ref,
        lambda hop: low_out_slots.at[hop - 1],
        low_out_send,
        low_out_recv,
    )
    value_copies = [
        send_to(
            "ctx",
            jnp.maximum(place - hop, 0),
            value_win_ref.at[(3 - hop) * row_count : (4 - hop) * row_count, :],
            value_slots.at[hop - 1],
            value_send.at[hop - 1],
            value_recv.at[hop - 1],
        )
        for hop in range(1, 4)
    ]
    for hop in (3, 2, 1):

        @pl.when(place >= hop)
        def _():
            value_copies[hop - 1].start()

    for hop in range(1, 4):

        @pl.when(place + hop >= ctx_size)
        def _():
            value_slots[hop - 1] = jnp.zeros(value_slots.shape[1:], value_slots.dtype)

    def columns(own, part):
        share = own.shape[1] // ctx_size
        return pl.ds(pl.multiple_of(part * share, 128), share)

    def scatter(own, slots, sends, recvs):
        return send_round(
            "ctx",
            lambda peer: own.at[:, columns(own, peer)],
            lambda hop: slots.at[hop - 1],
            sends,
            recvs,
        )

    def gather(own, copies, slots, part, total, sends, recvs):
        mine = columns(own, place)
        part[...] = slot_total(own[:, mine], copies, slots).astype(jnp.bfloat16)
        total[:, mine] = part[...]
        return send_round(
            "ctx", lambda peer: part, lambda hop: total.at[:, mine], sends, recvs
        )

    def gathered(copies, total, recvs):
        for hop, copy in enumerate(copies):
            peer = (place + ctx_size - hop - 1) % ctx_size
            send_to(
                "ctx", (place + 1) % ctx_size, total.at[:, columns(total, peer)],
                total.at[:, columns(total, peer)], recvs.at[hop], recvs.at[hop],
            ).wait_recv()

    if first_own.shape[1] > 2 * width:
        first_own[:, 2 * width :] = jnp.zeros(
            (first_own.shape[0], first_own.shape[1] - 2 * width), jnp.bfloat16
        )
    if second_own.shape[1] > width + kv_width:
        second_own[:, width + kv_width :] = jnp.zeros(
            (second_own.shape[0], second_own.shape[1] - width - kv_width), jnp.bfloat16
        )
    first_own[:, 0:width] = down_grad_ref[...].astype(jnp.bfloat16)
    low_o = slot_total(low_out_ref[...], low_out_copies, low_out_slots).astype(jnp.bfloat16)
    low_o_ref[...] = low_o
    weighted = (ADAPTER_SCALE * weight_ref[...] * low_o.astype(jnp.float32)).astype(jnp.bfloat16)
    loads[0].wait()
    first_own[:, width : 2 * width] = jnp.dot(
        weighted, cot[...], preferred_element_type=jnp.float32
    ).astype(jnp.bfloat16)
    first_copies = scatter(first_own, first_slots, first_send, first_recv)
    total = value_win_ref[3 * row_count : 4 * row_count, :].astype(jnp.float32)
    for hop in range(1, 4):

        @pl.when(place + hop < ctx_size)
        def _():
            value_copies[hop - 1].wait_recv()

        total = total + value_slots[hop - 1].astype(jnp.float32)
    value_grad = total.astype(jnp.bfloat16)
    low_grad_own[...] = ADAPTER_SCALE * score_block(value_up_ref[...], value_grad)
    low_grad_copies = send_round(
        "tp",
        lambda peer: low_grad_own,
        lambda hop: low_grad_slots.at[hop - 1],
        low_grad_send,
        low_grad_recv,
    )
    second_own[:, width : width + kv_width] = (
        ADAPTER_SCALE * jnp.dot(low_v_ref[...], value_grad, preferred_element_type=jnp.float32)
    ).astype(jnp.bfloat16)
    first_back = gather(
        first_own, first_copies, first_slots, first_part, first_sum, first_back_send, first_back_recv
    )
    low_grad = slot_total(low_grad_own[...], low_grad_copies, low_grad_slots).astype(jnp.bfloat16)
    low_v_grad_ref[...] = low_grad
    loads[1].wait()
    second_own[:, 0:width] = jnp.dot(
        low_grad, hidden[...], preferred_element_type=jnp.float32
    ).astype(jnp.bfloat16)
    second_copies = scatter(second_own, second_slots, second_send, second_recv)
    gathered(first_back, first_sum, first_back_recv)
    output_down_ref[...] = first_sum[:, 0:width].astype(jnp.float32)
    output_up_ref[...] = first_sum[:, width : 2 * width].astype(jnp.float32)
    second_back = gather(
        second_own,
        second_copies,
        second_slots,
        second_part,
        second_sum,
        second_back_send,
        second_back_recv,
    )
    gathered(second_back, second_sum, second_back_recv)
    value_down_ref[...] = second_sum[:, 0:width].astype(jnp.float32)
    value_up_grad_ref[...] = second_sum[:, width : width + kv_width].astype(jnp.float32)
    for hop in range(1, 4):

        @pl.when(place >= hop)
        def _():
            value_copies[hop - 1].wait_send()

    for copies in (
        low_out_copies,
        low_grad_copies,
        first_copies,
        first_back,
        second_copies,
        second_back,
    ):
        for copy in copies:
            copy.wait_send()


def finish(value_win, low_out, hidden, cot, value_up, low_v, weight, down_grad):
    row_count, width = hidden.shape
    kv_width = value_win.shape[1]
    rank = low_out.shape[0]
    ctx_size, tp_size = lax.axis_size("ctx"), lax.axis_size("tp")
    first_share = -(-2 * width // (128 * ctx_size)) * 128
    second_share = -(-(width + kv_width) // (128 * ctx_size)) * 128
    whole = pl.BlockSpec(memory_space=pltpu.VMEM)
    far = pl.BlockSpec(memory_space=pl.ANY)
    f32, bf16 = jnp.float32, jnp.bfloat16

    def reduction(share):
        return [
            pltpu.VMEM((rank, share * ctx_size), bf16),
            pltpu.VMEM((ctx_size - 1, rank, share), bf16),
            pltpu.VMEM((rank, share), bf16),
            pltpu.VMEM((rank, share * ctx_size), bf16),
        ]

    return pl.pallas_call(
        finish_kernel,
        in_specs=[whole, whole, far, far] + [whole] * 4,
        out_specs=[whole] * 6,
        out_shape=[
            jax.ShapeDtypeStruct((rank, row_count), bf16),
            jax.ShapeDtypeStruct((rank, row_count), bf16),
            jax.ShapeDtypeStruct((rank, width), f32),
            jax.ShapeDtypeStruct((rank, kv_width), f32),
            jax.ShapeDtypeStruct((rank, width), f32),
            jax.ShapeDtypeStruct((rank, width), f32),
        ],
        scratch_shapes=[
            pltpu.VMEM(hidden.shape, bf16),
            pltpu.VMEM(cot.shape, bf16),
            pltpu.VMEM((3, row_count, kv_width), bf16),
            pltpu.VMEM((tp_size - 1, rank, row_count), f32),
            pltpu.VMEM((rank, row_count), f32),
            pltpu.VMEM((tp_size - 1, rank, row_count), f32),
            *reduction(first_share),
            *reduction(second_share),
            dma_sems(3),
            dma_sems(3),
            *[dma_sems(tp_size - 1)] * 4,
            *[dma_sems(ctx_size - 1)] * 8,
            dma_sems(2),
        ],
        compiler_params=pltpu.CompilerParams(
            collective_id=1, has_side_effects=True, vmem_limit_bytes=VMEM_LIMIT
        ),
    )(value_win, low_out, hidden, cot, value_up, low_v, weight, down_grad)


def expand_kernel(
    low_o_ref,
    low_v_grad_ref,
    up_ref,
    down_t_ref,
    value_down_ref,
    value_up_ref,
    output_down_ref,
    output_up_ref,
    term_ref,
    input_ref,
    value_down_out,
    value_up_out,
    output_down_out,
    output_up_out,
):
    term_ref[...] = (ADAPTER_SCALE * row_contraction(low_o_ref[...], up_ref[...])).astype(
        jnp.bfloat16
    )
    input_ref[...] = row_contraction(low_v_grad_ref[...], down_t_ref[...]).astype(jnp.bfloat16)
    value_down_out[...] = value_down_ref[...]
    value_up_out[...] = value_up_ref[...]
    output_down_out[...] = output_down_ref[...]
    output_up_out[...] = output_up_ref[...]


def expand(low_o, low_v_grad, up, down_t, value_down, value_up, output_down, output_up):
    rank, width = up.shape
    row_count = low_o.shape[1]
    block = width // 4
    whole = lambda shape: pl.BlockSpec(shape, lambda i: (0, 0))
    wide = pl.BlockSpec((row_count, block), lambda i: (0, i))
    thin = pl.BlockSpec((rank, block), lambda i: (0, i))
    rows = jax.ShapeDtypeStruct((row_count, width), jnp.bfloat16)
    grad = jax.ShapeDtypeStruct((rank, width), jnp.float32)
    return pl.pallas_call(
        expand_kernel,
        grid=(4,),
        in_specs=[whole(low_o.shape)] * 2 + [thin] * 3 + [whole(value_up.shape)] + [thin] * 2,
        out_specs=[wide, wide, thin, whole(value_up.shape), thin, thin],
        out_shape=[rows, rows, grad, jax.ShapeDtypeStruct(value_up.shape, jnp.float32), grad, grad],
        compiler_params=pltpu.CompilerParams(vmem_limit_bytes=VMEM_LIMIT),
    )(low_o, low_v_grad, up, down_t, value_down, value_up, output_down, output_up)


def shards(
    hidden,
    queries,
    rotated_keys,
    frozen_value_rows,
    adapter_a_v,
    value_up_matrix,
    adapter_a_o,
    output_up_matrix,
    doc_lengths,
    pair_slots,
    token_logratio,
    out_cotangent,
    attn_cotangent,
):
    key_window, value_window, low_v_t, low_grad_t, weight, weight_rows, starts = begin(
        hidden,
        adapter_a_v.T,
        out_cotangent,
        output_up_matrix,
        rotated_keys,
        frozen_value_rows,
        value_up_matrix,
        token_logratio[None, :],
        doc_lengths[None, :],
        pair_slots[None, :],
    )
    attention_output_rows, value_terms, low_out_t, down_grad_t = attention(
        doc_lengths,
        queries,
        key_window,
        value_window,
        attn_cotangent,
        weight_rows,
        low_grad_t,
        adapter_a_o.T,
        starts,
    )
    finished = finish(
        value_terms,
        low_out_t,
        hidden,
        out_cotangent,
        value_up_matrix,
        low_v_t,
        weight,
        down_grad_t,
    )
    low_o_t, low_v_grad_t = finished[:2]
    (
        output_adapter_term,
        input_adapter_gradient,
        value_down_t,
        value_up_gradient,
        output_down_t,
        output_up_gradient,
    ) = expand(low_o_t, low_v_grad_t, output_up_matrix, adapter_a_v.T, *finished[2:])
    return (
        attention_output_rows,
        output_adapter_term,
        input_adapter_gradient,
        value_down_t.T,
        value_up_gradient,
        output_down_t.T,
        output_up_gradient,
    )


def solution(mesh):
    in_specs = (
        P("ctx", "tp"),
        P("ctx", "tp"),
        P("ctx", "tp"),
        P("ctx", "tp"),
        P("tp", None),
        P(None, "tp"),
        P("tp", None),
        P(None, "tp"),
        P(),
        P(),
        P("ctx"),
        P("ctx", "tp"),
        P("ctx", "tp"),
    )
    out_specs = (
        P("ctx", "tp"),
        P("ctx", "tp"),
        P("ctx", "tp"),
        P("tp", None),
        P(None, "tp"),
        P("tp", None),
        P(None, "tp"),
    )
    return jax.shard_map(shards, mesh=mesh, in_specs=in_specs, out_specs=out_specs, check_vma=False)
```

```python
import math

import jax
import jax.numpy as jnp
from jax import lax
from jax.experimental import pallas as pl
from jax.experimental.pallas import tpu as pltpu
from jax.sharding import PartitionSpec as P

HEADS = 64
KV_HEADS = 8
HD = 128


ADAPTER_SCALE = 2.0
BETA = 0.5
NEG_FILL = -1e30


def score_block(left, right):
    return lax.dot_general(
        left, right, (((1,), (1,)), ((), ())), preferred_element_type=jnp.float32
    )


def row_contraction(left, right):
    return lax.dot_general(
        left, right, (((0,), (0,)), ((), ())), preferred_element_type=jnp.float32
    )

TILE = 256
STEP_HEADS = 4
VMEM_LIMIT = 58 * 1024 * 1024
EXP2_SCALE = 1.4426950408889634 / math.sqrt(HD)


def attention_kernel(
    lengths_ref,
    query_ref,
    key_ref,
    value_ref,
    cot_ref,
    weight_ref,
    low_grad_t_ref,
    down_t_ref,
    start_ref,
    out_ref,
    value_grad_ref,
    low_out_ref,
    down_grad_ref,
    bias,
    scores,
    weights,
    grads,
    value_t,
    value_acc,
):
    step = pl.program_id(0)
    steps_per_kv = HEADS // KV_HEADS // STEP_HEADS
    row_count = query_ref.shape[0]
    window = key_ref.shape[0]
    tiles = window // TILE
    query_tiles = row_count // TILE

    first_row = lax.axis_index("ctx") * row_count

    def tile_reach(qt):
        position = first_row + qt * TILE

        def pass_doc(doc, carried):
            end = carried[0] + lengths_ref[doc]
            return end, jnp.where(end <= position, end, carried[1])

        zero = jnp.int32(0)
        start = lax.fori_loop(0, lengths_ref.shape[0], pass_doc, (zero, zero))[1]
        first = (start - first_row + window - row_count) // TILE
        return first, (window - row_count) // TILE + qt - first + 1

    @pl.when(step == 0)
    def _():
        low_out_ref[...] = jnp.zeros_like(low_out_ref)

        @pl.loop(0, query_tiles)
        def _(qt):
            first, count = tile_reach(qt)
            lane = pl.ds(pl.multiple_of(qt * TILE, TILE), TILE)
            starts = start_ref[:, lane]
            query_pos = (
                window - row_count + qt * TILE + lax.broadcasted_iota(jnp.int32, (1, TILE), 1)
            )

            @pl.loop(0, count)
            def _(k):
                key_pos = (first + k) * TILE + lax.broadcasted_iota(
                    jnp.int32, (TILE, TILE), 0
                )
                allowed = (key_pos >= starts) & (key_pos <= query_pos)
                rows = pl.ds(pl.multiple_of(k * TILE, TILE), TILE)
                bias[qt, rows, :] = jnp.where(allowed, 0.0, NEG_FILL)

    @pl.when(step % steps_per_kv == 0)
    def _():
        value_acc[...] = jnp.zeros_like(value_acc)
        for k in range(tiles):
            rows = slice(k * TILE, (k + 1) * TILE)
            value_t[:, rows] = jnp.transpose(value_ref[rows, :].astype(jnp.float32)).astype(
                jnp.bfloat16
            )

    def heads(qt, first, count):
        rows = pl.ds(pl.multiple_of(qt * TILE, TILE), TILE)
        columns = [slice(h * HD, (h + 1) * HD) for h in range(STEP_HEADS)]
        lanes = [slice(h * TILE, (h + 1) * TILE) for h in range(STEP_HEADS)]

        def key_rows(k):
            return pl.ds(pl.multiple_of((first + k) * TILE, TILE), TILE)

        tops = [jnp.full((8, TILE), NEG_FILL, jnp.float32)] * STEP_HEADS
        for k in range(count):
            span = slice(k * TILE, (k + 1) * TILE)
            for h in range(STEP_HEADS):
                block = (
                    score_block(key_ref[key_rows(k), :], query_ref[rows, columns[h]])
                    + bias[qt, span, :]
                )
                scores[span, lanes[h]] = block
                tops[h] = jnp.maximum(
                    tops[h], jnp.max(block.reshape(TILE // 8, 8, TILE), axis=0)
                )
        tops = [jnp.max(top, axis=0, keepdims=True) * EXP2_SCALE for top in tops]
        totals = [jnp.zeros((8, TILE), jnp.float32)] * STEP_HEADS
        for k in range(count):
            span = slice(k * TILE, (k + 1) * TILE)
            for h in range(STEP_HEADS):
                block = jnp.exp2(scores[span, lanes[h]] * EXP2_SCALE - tops[h])
                totals[h] = totals[h] + jnp.sum(block.reshape(TILE // 8, 8, TILE), axis=0)
                weights[span, lanes[h]] = block.astype(jnp.bfloat16)
        inverses = [1.0 / jnp.sum(total, axis=0, keepdims=True) for total in totals]
        for h in range(STEP_HEADS):
            inverse_rows = jnp.transpose(jnp.broadcast_to(inverses[h], (HD, TILE)))
            grad = weight_ref[rows, :] * cot_ref[rows, columns[h]].astype(
                jnp.float32
            ) + row_contraction(low_grad_t_ref[:, rows], down_t_ref[:, columns[h]])
            grads[lanes[h], :] = (grad * inverse_rows).astype(jnp.bfloat16)
        for h in range(STEP_HEADS):
            output = jnp.zeros((HD, TILE), jnp.float32)
            for k in range(count):
                span = slice(k * TILE, (k + 1) * TILE)
                output = output + jnp.dot(
                    value_t[:, key_rows(k)],
                    weights[span, lanes[h]],
                    preferred_element_type=jnp.float32,
                )
            out_ref[rows, columns[h]] = jnp.transpose(output * inverses[h]).astype(jnp.bfloat16)
        for k in range(count):
            span = slice(k * TILE, (k + 1) * TILE)
            value_acc[key_rows(k), :] += jnp.dot(
                weights[span, :], grads[...], preferred_element_type=jnp.float32
            )

    @pl.loop(0, query_tiles)
    def _(qt):
        first, count = tile_reach(qt)
        for variant in range(1, (window - row_count) // TILE + 2):

            @pl.when(count == variant)
            def _():
                heads(qt, first, variant)

    low_out_ref[...] += lax.dot_general(
        down_t_ref[...],
        out_ref[...],
        (((1,), (1,)), ((), ())),
        preferred_element_type=jnp.float32,
    )
    down_grad_ref[...] = jnp.dot(
        low_grad_t_ref[...], out_ref[...], preferred_element_type=jnp.float32
    )

    @pl.when(step % steps_per_kv == steps_per_kv - 1)
    def _():
        value_grad_ref[...] = value_acc[...].astype(value_grad_ref.dtype)


def attention(lengths, queries, keys, values, cot, weight, low_grad_t, down_t, starts):
    row_count, width = queries.shape
    window = keys.shape[0]
    rank = low_grad_t.shape[0]
    block = STEP_HEADS * HD
    steps = width // block
    steps_per_kv = HEADS // KV_HEADS // STEP_HEADS
    by_step = lambda i, lengths: (0, i)
    by_kv = lambda i, lengths: (0, i // steps_per_kv)
    whole = lambda i, lengths: (0, 0)
    return pl.pallas_call(
        attention_kernel,
        grid_spec=pltpu.PrefetchScalarGridSpec(
            num_scalar_prefetch=1,
            grid=(steps,),
            in_specs=[
                pl.BlockSpec((row_count, block), by_step),
                pl.BlockSpec((window, HD), by_kv),
                pl.BlockSpec((window, HD), by_kv),
                pl.BlockSpec((row_count, block), by_step),
                pl.BlockSpec((row_count, HD), whole),
                pl.BlockSpec((rank, row_count), whole),
                pl.BlockSpec((rank, block), by_step),
                pl.BlockSpec((1, row_count), whole),
            ],
            out_specs=[
                pl.BlockSpec((row_count, block), by_step),
                pl.BlockSpec((window, HD), by_kv),
                pl.BlockSpec((rank, row_count), whole),
                pl.BlockSpec((rank, block), by_step),
            ],
            scratch_shapes=[
                pltpu.VMEM((row_count // TILE, window, TILE), jnp.float32),
                pltpu.VMEM((window, STEP_HEADS * TILE), jnp.float32),
                pltpu.VMEM((window, STEP_HEADS * TILE), jnp.bfloat16),
                pltpu.VMEM((STEP_HEADS * TILE, HD), jnp.bfloat16),
                pltpu.VMEM((HD, window), jnp.bfloat16),
                pltpu.VMEM((window, HD), jnp.float32),
            ],
        ),
        out_shape=[
            jax.ShapeDtypeStruct((row_count, width), jnp.bfloat16),
            jax.ShapeDtypeStruct(keys.shape, jnp.bfloat16),
            jax.ShapeDtypeStruct((rank, row_count), jnp.float32),
            jax.ShapeDtypeStruct((rank, width), jnp.float32),
        ],
        compiler_params=pltpu.CompilerParams(vmem_limit_bytes=VMEM_LIMIT),
    )(lengths, queries, keys, values, cot, weight, low_grad_t, down_t, starts)


MESH = pl.DeviceIdType.MESH


def greet_all():
    barrier = pltpu.get_barrier_semaphore()
    count = 0
    for axis in ("ctx", "tp"):
        size = lax.axis_size(axis)
        place = lax.axis_index(axis)
        for hop in range(1, size):
            pl.semaphore_signal(
                barrier, inc=1, device_id={axis: (place + hop) % size}, device_id_type=MESH
            )
            count += 1
    pl.semaphore_wait(barrier, count)


def send_to(axis, place, source, target, send_sem, recv_sem):
    return pltpu.make_async_remote_copy(
        src_ref=source,
        dst_ref=target,
        send_sem=send_sem,
        recv_sem=recv_sem,
        device_id={axis: place},
        device_id_type=MESH,
    )


def send_round(axis, source, slots, send_sems, recv_sems):
    size = lax.axis_size(axis)
    place = lax.axis_index(axis)
    copies = []
    for hop in range(1, size):
        copy = send_to(
            axis,
            (place + hop) % size,
            source((place + hop) % size),
            slots(hop),
            send_sems.at[hop - 1],
            recv_sems.at[hop - 1],
        )
        copy.start()
        copies.append(copy)
    return copies


def slot_total(own, copies, slots):
    total = own.astype(jnp.float32)
    for hop, copy in enumerate(copies):
        copy.wait_recv()
        total = total + slots[hop].astype(jnp.float32)
    return total


def begin_kernel(
    hidden_ref,
    down_v_t_ref,
    cot_ref,
    up_ref,
    key_ref,
    frozen_ref,
    value_up_ref,
    ratio_ref,
    lengths_ref,
    slots_ref,
    key_win_ref,
    value_win_ref,
    low_v_ref,
    low_grad_ref,
    weight_ref,
    weight_rows_ref,
    start_ref,
    hidden,
    cot,
    pack,
    pack_slots,
    margin_own,
    margin_slots,
    frozen_slots,
    low_slots,
    pack_send,
    pack_recv,
    margin_send,
    margin_recv,
    rows_send,
    rows_recv,
    low_send,
    low_recv,
    load_sems,
):
    ctx_size = lax.axis_size("ctx")
    place = lax.axis_index("ctx")
    loads = [
        pltpu.make_async_copy(hidden_ref, hidden, load_sems.at[0]),
        pltpu.make_async_copy(cot_ref, cot, load_sems.at[1]),
    ]
    for load in loads:
        load.start()
    row_count = hidden_ref.shape[0]
    rank = down_v_t_ref.shape[0]
    odd = place % 2
    greet_all()

    def window_rows(slot):
        return pl.ds(pl.multiple_of(slot * row_count, row_count), row_count)

    def row_copies(sources, peer, slot, sem):
        targets = (key_win_ref.at[window_rows(slot), :], frozen_slots.at[slot])
        return [
            send_to(
                "ctx",
                jnp.minimum(peer, ctx_size - 1),
                sources[which],
                targets[which],
                rows_send.at[sem, which],
                rows_recv.at[slot, which],
            )
            for which in range(2)
        ]

    own = (key_ref, frozen_ref)
    near = row_copies(own, place + 1, 2, 0)
    far = row_copies(own, place + 2 + odd, 1 - odd, 1)
    near_on = place + 1 < ctx_size
    far_on = place + 2 + odd < ctx_size

    def passed_on(slot):
        sources = (key_win_ref.at[window_rows(slot), :], frozen_slots.at[slot])
        return row_copies(sources, place + 1, slot - 1, 1 + slot)

    def pass_on(slot):
        return (odd == 0) & near_on & (place >= 3 - slot)

    @pl.when(near_on)
    def _():
        for copy in near:
            copy.start()

    @pl.when(far_on)
    def _():
        for copy in far:
            copy.start()

    for slot in range(3):

        @pl.when(place < 3 - slot)
        def _():
            key_win_ref[slot * row_count : (slot + 1) * row_count, :] = jnp.zeros(
                key_ref.shape, key_ref.dtype
            )
            frozen_slots[slot] = jnp.zeros(frozen_ref.shape, frozen_ref.dtype)
            low_slots[slot] = jnp.zeros(low_v_ref.shape, low_v_ref.dtype)

    docs = lengths_ref.shape[1]
    by_row = lax.broadcasted_iota(jnp.int32, (docs, docs), 0)
    by_lane = lax.broadcasted_iota(jnp.int32, (docs, docs), 1)
    ends = jnp.sum(jnp.where(by_lane <= by_row, lengths_ref[...], 0), axis=1, keepdims=True)
    begins = jnp.sum(jnp.where(by_lane < by_row, lengths_ref[...], 0), axis=1, keepdims=True)
    positions = place * row_count + lax.broadcasted_iota(jnp.int32, (docs, row_count), 1)
    member = (positions >= begins) & (positions < ends)
    start_ref[...] = jnp.sum(jnp.where(member, begins, 0), axis=0, keepdims=True) - (
        place - 3
    ) * row_count
    margins = jnp.sum(jnp.where(member, ratio_ref[...], 0.0), axis=1, keepdims=True)
    margin_own[...] = jnp.broadcast_to(margins, margin_own.shape)
    margin_copies = send_round(
        "ctx", lambda peer: margin_own, lambda hop: margin_slots.at[hop - 1], margin_send, margin_recv
    )
    for load in loads:
        load.wait()
    pack[0:rank, :] = score_block(down_v_t_ref[...], hidden[...])
    pack[rank : 2 * rank, :] = score_block(up_ref[...], cot[...])
    pack_copies = send_round(
        "tp", lambda peer: pack, lambda hop: pack_slots.at[hop - 1], pack_send, pack_recv
    )
    key_win_ref[3 * row_count : 4 * row_count, :] = key_ref[...]
    sums = slot_total(pack[...], pack_copies, pack_slots)
    low_v_ref[...] = sums[0:rank, :].astype(jnp.bfloat16)
    low_copies = [
        send_to(
            "ctx",
            jnp.minimum(place + hop, ctx_size - 1),
            low_v_ref,
            low_slots.at[3 - hop],
            low_send.at[hop - 1],
            low_recv.at[hop - 1],
        )
        for hop in range(1, 4)
    ]
    for hop in range(1, 4):

        @pl.when(place + hop < ctx_size)
        def _():
            low_copies[hop - 1].start()

    for slot in (2, 1):

        @pl.when(pass_on(slot))
        def _():
            onward = passed_on(slot)
            for which in range(2):
                row_copies(own, place + 1, slot, 0)[which].wait_recv()
                onward[which].start()

    margins = slot_total(margin_own[...], margin_copies, margin_slots)[:, 0:1]
    slot_column = jnp.sum(jnp.where(by_row == by_lane, slots_ref[...], 0), axis=1, keepdims=True)
    sign_column = jnp.where(slot_column % 2 == 0, 1.0, -1.0)
    signed_row = jnp.sum(
        jnp.where(by_row == by_lane, sign_column * margins, 0.0), axis=0, keepdims=True
    )
    gaps = jnp.sum(
        jnp.where(slot_column // 2 == slots_ref[...] // 2, signed_row, 0.0), axis=1, keepdims=True
    )
    doc_weight = -BETA * sign_column * jax.nn.sigmoid(-BETA * gaps)
    weight = jnp.sum(jnp.where(member, doc_weight, 0.0), axis=0, keepdims=True)
    weight_ref[...] = weight
    weight_rows_ref[...] = jnp.transpose(jnp.broadcast_to(weight, (HD, row_count)))
    low_grad_ref[...] = (ADAPTER_SCALE * weight * sums[rank : 2 * rank, :]).astype(jnp.bfloat16)

    def rows_of(low, frozen):
        return (
            frozen.astype(jnp.float32) + ADAPTER_SCALE * row_contraction(low, value_up_ref[...])
        ).astype(jnp.bfloat16)

    value_win_ref[3 * row_count : 4 * row_count, :] = rows_of(low_v_ref[...], frozen_ref[...])
    for slot in (2, 1, 0):

        @pl.when(place >= 3 - slot)
        def _():
            low_copies[2 - slot].wait_recv()

        already = pass_on(slot) if slot > 0 else place < 0

        @pl.when((place >= 3 - slot) & jnp.logical_not(already))
        def _():
            for which in range(2):
                row_copies(own, place + 1, slot, 0)[which].wait_recv()

        value_win_ref[slot * row_count : (slot + 1) * row_count, :] = rows_of(
            low_slots[slot], frozen_slots[slot]
        )

    @pl.when(far_on)
    def _():
        for copy in far:
            copy.wait_send()

    @pl.when(near_on)
    def _():
        for copy in near:
            copy.wait_send()

    for slot in (2, 1):

        @pl.when(pass_on(slot))
        def _():
            for copy in passed_on(slot):
                copy.wait_send()

    for hop in range(1, 4):

        @pl.when(place + hop < ctx_size)
        def _():
            low_copies[hop - 1].wait_send()

    for copy in margin_copies + pack_copies:
        copy.wait_send()


def dma_sems(*shape):
    return pltpu.SemaphoreType.DMA(shape)


def begin(hidden, down_v_t, cot, up, keys, frozen, value_up, ratio, lengths, slots):
    row_count = hidden.shape[0]
    rank = up.shape[0]
    docs = lengths.shape[1]
    ctx_size, tp_size = lax.axis_size("ctx"), lax.axis_size("tp")
    window = (4 * row_count, keys.shape[1])
    whole = pl.BlockSpec(memory_space=pltpu.VMEM)
    far = pl.BlockSpec(memory_space=pl.ANY)
    f32, bf16 = jnp.float32, jnp.bfloat16
    return pl.pallas_call(
        begin_kernel,
        in_specs=[far, whole, far] + [whole] * 7,
        out_specs=[whole] * 7,
        out_shape=[
            jax.ShapeDtypeStruct(window, bf16),
            jax.ShapeDtypeStruct(window, bf16),
            jax.ShapeDtypeStruct((rank, row_count), bf16),
            jax.ShapeDtypeStruct((rank, row_count), bf16),
            jax.ShapeDtypeStruct((1, row_count), f32),
            jax.ShapeDtypeStruct((row_count, HD), f32),
            jax.ShapeDtypeStruct((1, row_count), jnp.int32),
        ],
        scratch_shapes=[
            pltpu.VMEM(hidden.shape, bf16),
            pltpu.VMEM(cot.shape, bf16),
            pltpu.VMEM((2 * rank, row_count), f32),
            pltpu.VMEM((tp_size - 1, 2 * rank, row_count), f32),
            pltpu.VMEM((docs, 128), f32),
            pltpu.VMEM((ctx_size - 1, docs, 128), f32),
            pltpu.VMEM((3, row_count, keys.shape[1]), bf16),
            pltpu.VMEM((3, rank, row_count), bf16),
            dma_sems(tp_size - 1),
            dma_sems(tp_size - 1),
            dma_sems(ctx_size - 1),
            dma_sems(ctx_size - 1),
            dma_sems(4, 2),
            dma_sems(3, 2),
            dma_sems(3),
            dma_sems(3),
            dma_sems(2),
        ],
        compiler_params=pltpu.CompilerParams(
            collective_id=0, has_side_effects=True, vmem_limit_bytes=VMEM_LIMIT
        ),
    )(hidden, down_v_t, cot, up, keys, frozen, value_up, ratio, lengths, slots)


def finish_kernel(
    value_win_ref,
    low_out_ref,
    hidden_ref,
    cot_ref,
    value_up_ref,
    low_v_ref,
    weight_ref,
    down_grad_ref,
    low_o_ref,
    low_v_grad_ref,
    value_down_ref,
    value_up_grad_ref,
    output_down_ref,
    output_up_ref,
    hidden,
    cot,
    value_slots,
    low_out_slots,
    low_grad_own,
    low_grad_slots,
    first_own,
    first_slots,
    first_part,
    first_sum,
    second_own,
    second_slots,
    second_part,
    second_sum,
    value_send,
    value_recv,
    low_out_send,
    low_out_recv,
    low_grad_send,
    low_grad_recv,
    first_send,
    first_recv,
    first_back_send,
    first_back_recv,
    second_send,
    second_recv,
    second_back_send,
    second_back_recv,
    load_sems,
):
    ctx_size = lax.axis_size("ctx")
    place = lax.axis_index("ctx")
    loads = [
        pltpu.make_async_copy(cot_ref, cot, load_sems.at[0]),
        pltpu.make_async_copy(hidden_ref, hidden, load_sems.at[1]),
    ]
    for load in loads:
        load.start()
    row_count, width = hidden_ref.shape
    kv_width = value_win_ref.shape[1]
    greet_all()
    low_out_copies = send_round(
        "tp",
        lambda peer: low_out_ref,
        lambda hop: low_out_slots.at[hop - 1],
        low_out_send,
        low_out_recv,
    )
    value_copies = [
        send_to(
            "ctx",
            jnp.maximum(place - hop, 0),
            value_win_ref.at[(3 - hop) * row_count : (4 - hop) * row_count, :],
            value_slots.at[hop - 1],
            value_send.at[hop - 1],
            value_recv.at[hop - 1],
        )
        for hop in range(1, 4)
    ]
    for hop in (3, 2, 1):

        @pl.when(place >= hop)
        def _():
            value_copies[hop - 1].start()

    for hop in range(1, 4):

        @pl.when(place + hop >= ctx_size)
        def _():
            value_slots[hop - 1] = jnp.zeros(value_slots.shape[1:], value_slots.dtype)

    def columns(own, part):
        share = own.shape[1] // ctx_size
        return pl.ds(pl.multiple_of(part * share, 128), share)

    def scatter(own, slots, sends, recvs):
        return send_round(
            "ctx",
            lambda peer: own.at[:, columns(own, peer)],
            lambda hop: slots.at[hop - 1],
            sends,
            recvs,
        )

    def gather(own, copies, slots, part, total, sends, recvs):
        mine = columns(own, place)
        part[...] = slot_total(own[:, mine], copies, slots).astype(jnp.bfloat16)
        total[:, mine] = part[...]
        return send_round(
            "ctx", lambda peer: part, lambda hop: total.at[:, mine], sends, recvs
        )

    def gathered(copies, total, recvs):
        for hop, copy in enumerate(copies):
            peer = (place + ctx_size - hop - 1) % ctx_size
            send_to(
                "ctx", (place + 1) % ctx_size, total.at[:, columns(total, peer)],
                total.at[:, columns(total, peer)], recvs.at[hop], recvs.at[hop],
            ).wait_recv()

    if first_own.shape[1] > 2 * width:
        first_own[:, 2 * width :] = jnp.zeros(
            (first_own.shape[0], first_own.shape[1] - 2 * width), jnp.bfloat16
        )
    if second_own.shape[1] > width + kv_width:
        second_own[:, width + kv_width :] = jnp.zeros(
            (second_own.shape[0], second_own.shape[1] - width - kv_width), jnp.bfloat16
        )
    first_own[:, 0:width] = down_grad_ref[...].astype(jnp.bfloat16)
    low_o = slot_total(low_out_ref[...], low_out_copies, low_out_slots).astype(jnp.bfloat16)
    low_o_ref[...] = low_o
    weighted = (ADAPTER_SCALE * weight_ref[...] * low_o.astype(jnp.float32)).astype(jnp.bfloat16)
    loads[0].wait()
    first_own[:, width : 2 * width] = jnp.dot(
        weighted, cot[...], preferred_element_type=jnp.float32
    ).astype(jnp.bfloat16)
    first_copies = scatter(first_own, first_slots, first_send, first_recv)
    total = value_win_ref[3 * row_count : 4 * row_count, :].astype(jnp.float32)
    for hop in range(1, 4):

        @pl.when(place + hop < ctx_size)
        def _():
            value_copies[hop - 1].wait_recv()

        total = total + value_slots[hop - 1].astype(jnp.float32)
    value_grad = total.astype(jnp.bfloat16)
    low_grad_own[...] = ADAPTER_SCALE * score_block(value_up_ref[...], value_grad)
    low_grad_copies = send_round(
        "tp",
        lambda peer: low_grad_own,
        lambda hop: low_grad_slots.at[hop - 1],
        low_grad_send,
        low_grad_recv,
    )
    second_own[:, width : width + kv_width] = (
        ADAPTER_SCALE * jnp.dot(low_v_ref[...], value_grad, preferred_element_type=jnp.float32)
    ).astype(jnp.bfloat16)
    first_back = gather(
        first_own, first_copies, first_slots, first_part, first_sum, first_back_send, first_back_recv
    )
    low_grad = slot_total(low_grad_own[...], low_grad_copies, low_grad_slots).astype(jnp.bfloat16)
    low_v_grad_ref[...] = low_grad
    loads[1].wait()
    second_own[:, 0:width] = jnp.dot(
        low_grad, hidden[...], preferred_element_type=jnp.float32
    ).astype(jnp.bfloat16)
    second_copies = scatter(second_own, second_slots, second_send, second_recv)
    gathered(first_back, first_sum, first_back_recv)
    output_down_ref[...] = first_sum[:, 0:width].astype(jnp.float32)
    output_up_ref[...] = first_sum[:, width : 2 * width].astype(jnp.float32)
    second_back = gather(
        second_own,
        second_copies,
        second_slots,
        second_part,
        second_sum,
        second_back_send,
        second_back_recv,
    )
    gathered(second_back, second_sum, second_back_recv)
    value_down_ref[...] = second_sum[:, 0:width].astype(jnp.float32)
    value_up_grad_ref[...] = second_sum[:, width : width + kv_width].astype(jnp.float32)
    for hop in range(1, 4):

        @pl.when(place >= hop)
        def _():
            value_copies[hop - 1].wait_send()

    for copies in (
        low_out_copies,
        low_grad_copies,
        first_copies,
        first_back,
        second_copies,
        second_back,
    ):
        for copy in copies:
            copy.wait_send()


def finish(value_win, low_out, hidden, cot, value_up, low_v, weight, down_grad):
    row_count, width = hidden.shape
    kv_width = value_win.shape[1]
    rank = low_out.shape[0]
    ctx_size, tp_size = lax.axis_size("ctx"), lax.axis_size("tp")
    first_share = -(-2 * width // (128 * ctx_size)) * 128
    second_share = -(-(width + kv_width) // (128 * ctx_size)) * 128
    whole = pl.BlockSpec(memory_space=pltpu.VMEM)
    far = pl.BlockSpec(memory_space=pl.ANY)
    f32, bf16 = jnp.float32, jnp.bfloat16

    def reduction(share):
        return [
            pltpu.VMEM((rank, share * ctx_size), bf16),
            pltpu.VMEM((ctx_size - 1, rank, share), bf16),
            pltpu.VMEM((rank, share), bf16),
            pltpu.VMEM((rank, share * ctx_size), bf16),
        ]

    return pl.pallas_call(
        finish_kernel,
        in_specs=[whole, whole, far, far] + [whole] * 4,
        out_specs=[whole] * 6,
        out_shape=[
            jax.ShapeDtypeStruct((rank, row_count), bf16),
            jax.ShapeDtypeStruct((rank, row_count), bf16),
            jax.ShapeDtypeStruct((rank, width), f32),
            jax.ShapeDtypeStruct((rank, kv_width), f32),
            jax.ShapeDtypeStruct((rank, width), f32),
            jax.ShapeDtypeStruct((rank, width), f32),
        ],
        scratch_shapes=[
            pltpu.VMEM(hidden.shape, bf16),
            pltpu.VMEM(cot.shape, bf16),
            pltpu.VMEM((3, row_count, kv_width), bf16),
            pltpu.VMEM((tp_size - 1, rank, row_count), f32),
            pltpu.VMEM((rank, row_count), f32),
            pltpu.VMEM((tp_size - 1, rank, row_count), f32),
            *reduction(first_share),
            *reduction(second_share),
            dma_sems(3),
            dma_sems(3),
            *[dma_sems(tp_size - 1)] * 4,
            *[dma_sems(ctx_size - 1)] * 8,
            dma_sems(2),
        ],
        compiler_params=pltpu.CompilerParams(
            collective_id=1, has_side_effects=True, vmem_limit_bytes=VMEM_LIMIT
        ),
    )(value_win, low_out, hidden, cot, value_up, low_v, weight, down_grad)


def expand_kernel(
    low_o_ref,
    low_v_grad_ref,
    up_ref,
    down_t_ref,
    value_down_ref,
    value_up_ref,
    output_down_ref,
    output_up_ref,
    term_ref,
    input_ref,
    value_down_out,
    value_up_out,
    output_down_out,
    output_up_out,
):
    term_ref[...] = (ADAPTER_SCALE * row_contraction(low_o_ref[...], up_ref[...])).astype(
        jnp.bfloat16
    )
    input_ref[...] = row_contraction(low_v_grad_ref[...], down_t_ref[...]).astype(jnp.bfloat16)
    value_down_out[...] = value_down_ref[...]
    value_up_out[...] = value_up_ref[...]
    output_down_out[...] = output_down_ref[...]
    output_up_out[...] = output_up_ref[...]


def expand(low_o, low_v_grad, up, down_t, value_down, value_up, output_down, output_up):
    rank, width = up.shape
    row_count = low_o.shape[1]
    block = width // 4
    whole = lambda shape: pl.BlockSpec(shape, lambda i: (0, 0))
    wide = pl.BlockSpec((row_count, block), lambda i: (0, i))
    thin = pl.BlockSpec((rank, block), lambda i: (0, i))
    rows = jax.ShapeDtypeStruct((row_count, width), jnp.bfloat16)
    grad = jax.ShapeDtypeStruct((rank, width), jnp.float32)
    return pl.pallas_call(
        expand_kernel,
        grid=(4,),
        in_specs=[whole(low_o.shape)] * 2 + [thin] * 3 + [whole(value_up.shape)] + [thin] * 2,
        out_specs=[wide, wide, thin, whole(value_up.shape), thin, thin],
        out_shape=[rows, rows, grad, jax.ShapeDtypeStruct(value_up.shape, jnp.float32), grad, grad],
        compiler_params=pltpu.CompilerParams(vmem_limit_bytes=VMEM_LIMIT),
    )(low_o, low_v_grad, up, down_t, value_down, value_up, output_down, output_up)


def shards(
    hidden,
    queries,
    rotated_keys,
    frozen_value_rows,
    adapter_a_v,
    value_up_matrix,
    adapter_a_o,
    output_up_matrix,
    doc_lengths,
    pair_slots,
    token_logratio,
    out_cotangent,
    attn_cotangent,
):
    key_window, value_window, low_v_t, low_grad_t, weight, weight_rows, starts = begin(
        hidden,
        adapter_a_v.T,
        out_cotangent,
        output_up_matrix,
        rotated_keys,
        frozen_value_rows,
        value_up_matrix,
        token_logratio[None, :],
        doc_lengths[None, :],
        pair_slots[None, :],
    )
    attention_output_rows, value_terms, low_out_t, down_grad_t = attention(
        doc_lengths,
        queries,
        key_window,
        value_window,
        attn_cotangent,
        weight_rows,
        low_grad_t,
        adapter_a_o.T,
        starts,
    )
    finished = finish(
        value_terms,
        low_out_t,
        hidden,
        out_cotangent,
        value_up_matrix,
        low_v_t,
        weight,
        down_grad_t,
    )
    low_o_t, low_v_grad_t = finished[:2]
    (
        output_adapter_term,
        input_adapter_gradient,
        value_down_t,
        value_up_gradient,
        output_down_t,
        output_up_gradient,
    ) = expand(low_o_t, low_v_grad_t, output_up_matrix, adapter_a_v.T, *finished[2:])
    return (
        attention_output_rows,
        output_adapter_term,
        input_adapter_gradient,
        value_down_t.T,
        value_up_gradient,
        output_down_t.T,
        output_up_gradient,
    )


def solution(mesh):
    in_specs = (
        P("ctx", "tp"),
        P("ctx", "tp"),
        P("ctx", "tp"),
        P("ctx", "tp"),
        P("tp", None),
        P(None, "tp"),
        P("tp", None),
        P(None, "tp"),
        P(),
        P(),
        P("ctx"),
        P("ctx", "tp"),
        P("ctx", "tp"),
    )
    out_specs = (
        P("ctx", "tp"),
        P("ctx", "tp"),
        P("ctx", "tp"),
        P("tp", None),
        P(None, "tp"),
        P("tp", None),
        P(None, "tp"),
    )
    return jax.shard_map(shards, mesh=mesh, in_specs=in_specs, out_specs=out_specs, check_vma=False)
```
